256 devices in a mesh: row: 8 (over x, y_hi), col: 32 (over z, y_lo, core).
Axes of the slice: x: 4, y: 4 (y_hi: 2, y_lo: 2; y = y_hi * 2 + y_lo), z: 8, core: 2. Of those that a mesh axis runs over, the one named last changes fastest.
Arguments:
- pair: bfloat16 [256, 256, 128], P('row', 'col'), may hold values from -6 to 6
- pair_mask: int32 [256, 256], P('row', 'col'), may hold values 0 or 1
- ln_in_gain: float32 [128], replicated, may hold values from 0.1 to 1.9
- w_ab: bfloat16 [128, 512], replicated, may hold values from -0.5 to 0.5
- w_gate: bfloat16 [128, 128], replicated, may hold values from -0.5 to 0.5
- ln_out_gain: float32 [128], replicated, may hold values from 0.1 to 1.9
- w_out: bfloat16 [128, 128], replicated, may hold values from -0.5 to 0.5
- cotangent: bfloat16 [256, 256, 128], P('row', 'col'), may hold values from -6 to 6
Outputs:
- update: bfloat16 [256, 256, 128], P('row', 'col')
- grad_pair: bfloat16 [256, 256, 128], P('row', 'col')
- grad_w_ab: float32 [128, 512], replicated
- grad_w_gate: float32 [128, 128], replicated
- grad_w_out: float32 [128, 128], replicated
The draws below stay inside these ranges and needn't reach their ends.
All inputs are finite; a program needn't handle non-finite values. No bound on the sum of `pair_mask` on one device may be relied on, other than what follows from the above.
Results may differ from the reference program's by a relative error of at most 0.025.
Values may be sent and summed in bfloat16 or wider, within the bound.
No kernel may reach another device: no remote copies, remote signals or barrier semaphores. Data moves between devices by JAX's collectives and lax.ppermute only.
A program may use at most 64 MiB of HBM per device.

```python
import jax
import jax.numpy as jnp
from jax import lax

C_Z = 128
C_H = 128
RES = 256


def plant(entries, own_key, smallest, largest):
    place = [jax.random.randint(jax.random.fold_in(own_key, axis), (), 0, length) for axis, length in enumerate(entries.shape)]
    widest = entries.shape.index(max(entries.shape))
    beside = place[:widest] + [(place[widest] + 1) % entries.shape[widest]] + place[widest + 1:]
    return entries.at[tuple(place)].set(smallest).at[tuple(beside)].set(largest)


def level_of(rng, extent, split, smallest, high):
    def one(dim, shards_of):
        draws = jax.random.uniform(jax.random.fold_in(jax.random.fold_in(rng, 6), dim), (shards_of,), jnp.float32, smallest / len(split), high / len(split))
        return jnp.repeat(jnp.exp(draws), extent[dim] // shards_of).reshape((-1,) + (1,) * (len(extent) - dim - 1))

    level = one(*split[0])
    for cut in split[1:]:
        level = level * one(*cut)
    return level


def bell_draw(rng, dims, width, reach, pieces=(), kind=jnp.bfloat16):
    entries = jax.random.normal(rng, dims, jnp.float32) * width
    if len(pieces) > 0:
        entries = level_of(rng, dims, pieces, -0.22, 0.18) * entries
    return jnp.clip(entries, min=-reach, max=reach).astype(kind)


def setup_inputs(seed: int = 0) -> dict:
    key_of = jax.random.split(jax.random.key(seed), 9)
    return {
        "pair": bell_draw(key_of[0], (RES, RES, C_Z), 1.0, 6.0, ((0, 8), (1, 32))),
        "pair_mask": plant((jax.random.randint(key_of[1], (RES, RES), 0, 8) < 7).astype(jnp.int32), jax.random.fold_in(key_of[1], 1), 0, 1),
        "ln_in_gain": jnp.clip(1.0 + 0.18 * jax.random.normal(key_of[2], (C_Z,), jnp.float32), 0.1, 1.9),
        "w_ab": bell_draw(key_of[3], (C_Z, 4 * C_H), C_Z ** -0.5, 0.5),
        "w_gate": bell_draw(key_of[4], (C_Z, C_Z), C_Z ** -0.5, 0.5),
        "ln_out_gain": jnp.clip(1.0 + 0.18 * jax.random.normal(key_of[5], (C_H,), jnp.float32), 0.1, 1.9),
        "w_out": bell_draw(key_of[6], (C_H, C_Z), C_H ** -0.5, 0.5),
        "cotangent": bell_draw(key_of[7], (RES, RES, C_Z), 1.0, 6.0, ((0, 8), (1, 32))),
    }


def layer_norm(values):
    center = values - lax.optimization_barrier(jnp.mean(values, axis=-1, keepdims=True))
    inverse = lax.rsqrt(lax.optimization_barrier(jnp.mean(center * center, axis=-1, keepdims=True)) + 1e-05)
    return (center * inverse, inverse)

def norm_back(grad_h, normed, inverse):
    first = lax.optimization_barrier(jnp.mean(grad_h, axis=-1, keepdims=True))
    second = lax.optimization_barrier(jnp.mean(grad_h * normed, axis=-1, keepdims=True))
    return inverse * (grad_h - first - normed * second)

def widen(values):
    return lax.optimization_barrier(values).astype(jnp.float32)

def reference(pair, pair_mask, ln_in_gain, w_ab, w_gate, ln_out_gain, w_out, cotangent):
    flat_pairs = RES * RES
    h_in, inv_in = layer_norm(pair.astype(jnp.float32))
    normed_in = (h_in * ln_in_gain).astype(jnp.bfloat16)
    flat_in = normed_in.reshape(flat_pairs, C_Z)
    proj = jnp.dot(flat_in, w_ab, preferred_element_type=jnp.float32).reshape(RES, RES, 4 * C_H)
    a_gate = proj[..., 0:C_H]
    a_value = proj[..., C_H:2 * C_H]
    b_gate = proj[..., 2 * C_H:3 * C_H]
    b_value = proj[..., 3 * C_H:4 * C_H]
    mask_f = pair_mask.astype(jnp.float32)[..., None]
    sig_a = jax.nn.sigmoid(a_gate)
    sig_b = jax.nn.sigmoid(b_gate)
    a_rows = (mask_f * sig_a * a_value).astype(jnp.bfloat16)
    b_rows = (mask_f * sig_b * b_value).astype(jnp.bfloat16)
    gate = jax.nn.sigmoid(jnp.dot(flat_in, w_gate, preferred_element_type=jnp.float32)).reshape(RES, RES, C_Z)
    a_wide = widen(a_rows)
    b_wide = widen(b_rows)
    mixed = jnp.einsum('ikc,jkc->ijc', a_wide, b_wide, precision=lax.Precision.HIGHEST)
    h_out, inv_out = layer_norm(mixed)
    normed_out = (h_out * ln_out_gain).astype(jnp.bfloat16)
    flat_out = normed_out.reshape(flat_pairs, C_H)
    y_val = jnp.dot(flat_out, w_out, preferred_element_type=jnp.float32).reshape(RES, RES, C_Z)
    update = (gate * y_val).astype(jnp.bfloat16)
    cot_f32 = cotangent.astype(jnp.float32)
    d_y = (cot_f32 * gate).astype(jnp.bfloat16).reshape(flat_pairs, C_Z)
    d_gate = (cot_f32 * y_val * gate * (1.0 - gate)).astype(jnp.bfloat16).reshape(flat_pairs, C_Z)
    grad_w_out = jnp.dot(flat_out.T, d_y, preferred_element_type=jnp.float32) / RES
    d_normed = jnp.dot(d_y, w_out.T, preferred_element_type=jnp.float32).reshape(RES, RES, C_H)
    d_mixed = norm_back(d_normed * ln_out_gain, h_out, inv_out).astype(jnp.bfloat16)
    d_wide = widen(d_mixed)
    d_a = jnp.einsum('ijc,jkc->ikc', d_wide, b_wide, precision=lax.Precision.HIGHEST)
    d_b = jnp.einsum('ijc,ikc->jkc', d_wide, a_wide, precision=lax.Precision.HIGHEST)
    d_a_value = d_a * mask_f * sig_a
    d_a_gate = d_a * mask_f * a_value * sig_a * (1.0 - sig_a)
    d_b_value = d_b * mask_f * sig_b
    d_b_gate = d_b * mask_f * b_value * sig_b * (1.0 - sig_b)
    d_proj = jnp.concatenate([d_a_gate, d_a_value, d_b_gate, d_b_value], axis=-1).astype(jnp.bfloat16)
    d_proj = d_proj.reshape(flat_pairs, 4 * C_H)
    grad_w_ab = jnp.dot(flat_in.T, d_proj, preferred_element_type=jnp.float32) / RES
    grad_w_gate = jnp.dot(flat_in.T, d_gate, preferred_element_type=jnp.float32) / RES
    d_in = jnp.dot(d_proj, w_ab.T, preferred_element_type=jnp.float32)
    d_in = d_in + jnp.dot(d_gate, w_gate.T, preferred_element_type=jnp.float32)
    d_in = d_in.reshape(RES, RES, C_Z)
    grad_pair = norm_back(d_in * ln_in_gain, h_in, inv_in).astype(jnp.bfloat16)
    return (update, grad_pair, grad_w_ab, grad_w_gate, grad_w_out)
```

```python
import jax
import jax.numpy as jnp
from jax import lax
from jax.experimental import pallas as pl
from jax.experimental.pallas import tpu as pltpu
from jax.sharding import PartitionSpec as P

F32 = jnp.float32
BF16 = jnp.bfloat16

ROWS, COLS, WIDTH = 32, 8, 128
NROW, NCOL = 8, 32
PAIRS = ROWS * COLS
GROUP = WIDTH // NCOL
RES = 256


def dot(left, right, left_dim, right_dim):
    return lax.dot_general(
        left, right, (((left_dim,), (right_dim,)), ((), ())), preferred_element_type=F32
    )


def lane_block(shape):
    return lax.broadcasted_iota(jnp.int32, shape, 1) // ROWS


def load_pairs(block, scratch):
    scratch[...] = block[...].astype(F32).reshape(PAIRS, WIDTH)
    return jnp.concatenate(
        [scratch[pl.ds(k, ROWS, stride=COLS), :] for k in range(COLS)], axis=0
    )


def store_pairs(values, scratch, block):
    for k in range(COLS):
        scratch[pl.ds(k, ROWS, stride=COLS), :] = values[k * ROWS : (k + 1) * ROWS]
    block[...] = scratch[...].reshape(ROWS, COLS, WIDTH).astype(block.dtype)


def regroup(scratch, blocks):
    return jnp.concatenate(
        [
            scratch[pl.ds(blk * WIDTH + c4, NCOL, stride=GROUP), :]
            for blk in range(blocks)
            for c4 in range(GROUP)
        ],
        axis=0,
    )


def ungroup(values, scratch, blocks):
    for blk in range(blocks):
        for c4 in range(GROUP):
            start = blk * WIDTH + c4 * NCOL
            scratch[pl.ds(blk * WIDTH + c4, NCOL, stride=GROUP), :] = values[start : start + NCOL]


def to_message(values, k):
    tile, place = k // GROUP, k % GROUP
    block = lane_block((NCOL, WIDTH))
    result = None
    for c4 in range(GROUP):
        part = values[c4 * NCOL : (c4 + 1) * NCOL, tile * WIDTH : (tile + 1) * WIDTH]
        shift = (c4 - place) * ROWS % WIDTH
        if shift:
            part = pltpu.roll(part, shift, 1)
        result = part if result is None else jnp.where(block == c4, part, result)
    return result


def from_message(pieces):
    block = lane_block((NCOL, WIDTH))
    bands = []
    for c4 in range(GROUP):
        tiles = []
        for tile in range(COLS // GROUP):
            result = None
            for place in range(GROUP):
                part = pieces[tile * GROUP + place]
                shift = (place - c4) * ROWS % WIDTH
                if shift:
                    part = pltpu.roll(part, shift, 1)
                result = part if result is None else jnp.where(block == place, part, result)
            tiles.append(result)
        bands.append(jnp.concatenate(tiles, axis=1))
    return jnp.concatenate(bands, axis=0)


def mask_rows(mask):
    flags = mask[...].astype(F32).astype(BF16)
    eye = (
        lax.broadcasted_iota(jnp.int32, (COLS, COLS), 0)
        == lax.broadcasted_iota(jnp.int32, (COLS, COLS), 1)
    ).astype(F32).astype(BF16)
    turned = dot(eye, flags, 1, 1).astype(BF16)
    spread = (
        lax.broadcasted_iota(jnp.int32, (ROWS, WIDTH), 1) % ROWS
        == lax.broadcasted_iota(jnp.int32, (ROWS, WIDTH), 0)
    ).astype(F32).astype(BF16)
    return dot(turned, spread, 1, 0)


def column_of(gain):
    row = lax.broadcasted_iota(jnp.int32, (WIDTH, WIDTH), 0)
    lane = lax.broadcasted_iota(jnp.int32, (WIDTH, WIDTH), 1)
    here = lane == (row % NCOL) * GROUP + row // NCOL
    return jnp.sum(jnp.where(here, gain, 0.0), axis=1, keepdims=True)


def layer_norm(values, axis):
    center = values - jnp.mean(values, axis=axis, keepdims=True)
    inverse = lax.rsqrt(jnp.mean(center * center, axis=axis, keepdims=True) + 1e-05)
    return center * inverse, inverse


def norm_back(grad_h, normed, inverse, axis):
    first = jnp.mean(grad_h, axis=axis, keepdims=True)
    second = jnp.mean(grad_h * normed, axis=axis, keepdims=True)
    return inverse * (grad_h - first - normed * second)


def halves(message):
    wide = message.astype(F32).reshape(NCOL, 2 * COLS, WIDTH)
    return wide[:, :COLS].reshape(PAIRS, WIDTH), wide[:, COLS:].reshape(PAIRS, WIDTH)


def project_kernel(pair, mask, gain, w_ab, normed_out, send, rows, weights, message):
    values = load_pairs(pair, rows)
    h_in, _ = layer_norm(values, 1)
    normed = (h_in * gain[...]).astype(BF16)
    normed_out[...] = normed
    weights[...] = w_ab[...].astype(F32).T
    proj = dot(regroup(weights, 4).astype(BF16), normed, 1, 1)
    a_val = jax.nn.sigmoid(proj[0:128]) * proj[128:256]
    b_val = jax.nn.sigmoid(proj[256:384]) * proj[384:512]
    flags = mask_rows(mask)
    for k in range(COLS):
        flag = flags[k : k + 1]
        message[pl.ds(k, NCOL, stride=2 * COLS), :] = to_message(a_val, k) * flag
        message[pl.ds(COLS + k, NCOL, stride=2 * COLS), :] = to_message(b_val, k) * flag
    send[...] = message[...].astype(BF16)


def mix_kernel(recv, b_all, send):
    a_val = halves(recv[...])[0].astype(BF16)
    block = lane_block((ROWS, WIDTH))
    for r in range(NROW):
        full = dot(b_all[r * RES : (r + 1) * RES], a_val, 0, 0)
        own = full[0:ROWS]
        for c4 in range(1, GROUP):
            own = jnp.where(block == c4, full[c4 * ROWS : (c4 + 1) * ROWS], own)
        send[r * ROWS : (r + 1) * ROWS] = own


def middle_kernel(
    recv, normed_in, cotangent, w_gate, gain, w_out,
    update, send, d_gate_out, grad_gate, grad_out, rows, weights,
):
    mixed = from_message([recv[pl.ds(k, NCOL, stride=COLS), :] for k in range(COLS)])
    h_out, inv_out = layer_norm(mixed, 0)
    scale = column_of(gain[...])
    normed = (h_out * scale).astype(BF16)
    weights[...] = w_out[...].astype(F32)
    w_own = regroup(weights, 1).astype(BF16)
    y_val = dot(normed, w_own, 0, 0)
    flat_in = normed_in[...]
    gate = jax.nn.sigmoid(dot(flat_in, w_gate[...], 1, 0))
    store_pairs(gate * y_val, rows, update)
    cot = load_pairs(cotangent, rows)
    d_y = (cot * gate).astype(BF16)
    d_gate = (cot * y_val * gate * (1.0 - gate)).astype(BF16)
    d_gate_out[...] = d_gate
    ungroup(dot(normed, d_y, 1, 0), weights, 1)
    grad_out[...] = weights[...]
    grad_gate[...] = dot(flat_in, d_gate, 0, 0)
    grad_h = dot(w_own, d_y, 1, 1) * scale
    d_mixed = norm_back(grad_h, h_out, inv_out, 0)
    for k in range(COLS):
        rows[pl.ds(k, NCOL, stride=COLS), :] = to_message(d_mixed, k)
    send[...] = rows[...].astype(BF16)


def grad_kernel(recv, b_all, d_mixed, d_a, d_b):
    a_val = halves(recv[...])[0].astype(BF16)
    own = (
        lax.broadcasted_iota(jnp.int32, (WIDTH, WIDTH), 0) // ROWS
        == lane_block((WIDTH, WIDTH))
    )
    total = None
    for r in range(NROW):
        part = d_mixed[r * ROWS : (r + 1) * ROWS].astype(F32)
        spread = jnp.where(own, jnp.concatenate([part] * GROUP, axis=0), 0.0).astype(BF16)
        term = dot(b_all[r * RES : (r + 1) * RES], spread, 1, 0)
        total = term if total is None else total + term
        d_b[r * RES : (r + 1) * RES] = dot(a_val, spread, 1, 1).astype(BF16)
    d_a[...] = total


def join_kernel(d_a, d_b, send):
    total = d_b[0:RES].astype(F32)
    for r in range(1, NROW):
        total = total + d_b[r * RES : (r + 1) * RES].astype(F32)
    both = jnp.concatenate(
        [d_a[...].reshape(NCOL, COLS, WIDTH), total.reshape(NCOL, COLS, WIDTH)], axis=1
    )
    send[...] = both.reshape(2 * PAIRS, WIDTH).astype(BF16)


def last_kernel(
    recv, pair, mask, gain, w_ab, w_gate, normed_in, d_gate,
    grad_pair, grad_ab, rows, weights, message,
):
    values = load_pairs(pair, rows)
    h_in, inv_in = layer_norm(values, 1)
    flat_in = normed_in[...]
    weights[...] = w_ab[...].astype(F32).T
    w_own = regroup(weights, 4).astype(BF16)
    proj = dot(w_own, flat_in, 1, 1)
    flags = mask_rows(mask)
    message[...] = recv[...].astype(F32)
    grads = []
    for half in range(2):
        pieces = [
            message[pl.ds(half * COLS + k, NCOL, stride=2 * COLS), :] * flags[k : k + 1]
            for k in range(COLS)
        ]
        d_val = from_message(pieces)
        sig = jax.nn.sigmoid(proj[half * 256 : half * 256 + 128])
        value = proj[half * 256 + 128 : half * 256 + 256]
        d_value = d_val * sig
        grads += [d_value * value * (1.0 - sig), d_value]
    d_proj = jnp.concatenate(grads, axis=0).astype(BF16)
    d_in = dot(d_proj, w_own, 0, 0) + dot(d_gate[...], w_gate[...], 1, 1)
    store_pairs(norm_back(d_in * gain[...], h_in, inv_in, 1), rows, grad_pair)
    ungroup(dot(d_proj, flat_in, 1, 0), weights, 4)
    grad_ab[...] = weights[...]


def call(kernel, outs, scratch, *args):
    return pl.pallas_call(
        kernel,
        out_shape=[jax.ShapeDtypeStruct(shape, dtype) for shape, dtype in outs],
        scratch_shapes=[pltpu.VMEM(shape, F32) for shape in scratch],
        compiler_params=pltpu.CompilerParams(vmem_limit_bytes=32 * 1024 * 1024),
    )(*args)


def exchange(values, axis):
    return lax.all_to_all(values, axis, 0, 0, tiled=True)


def on_device(pair, pair_mask, ln_in_gain, w_ab, w_gate, ln_out_gain, w_out, cotangent):
    gain_in = ln_in_gain.reshape(1, WIDTH)
    gain_out = ln_out_gain.reshape(1, WIDTH)
    flat = (PAIRS, WIDTH)
    twice = (2 * PAIRS, WIDTH)
    copies = (NROW * RES, WIDTH)
    blocks = (ROWS, COLS, WIDTH)
    normed_in, send_ab = call(
        project_kernel,
        [(flat, BF16), (twice, BF16)],
        [flat, (4 * WIDTH, WIDTH), twice],
        pair, pair_mask, gain_in, w_ab,
    )
    recv_ab = exchange(send_ab, "col")
    b_own = recv_ab.reshape(NCOL, 2 * COLS, WIDTH)[:, COLS:].reshape(flat)
    b_all = exchange(jnp.broadcast_to(b_own[None], (NROW,) + flat).reshape(copies), "row")
    (send_mixed,) = call(mix_kernel, [(flat, F32)], [], recv_ab, b_all)
    recv_mixed = exchange(send_mixed, "col")
    update, send_d, d_gate, grad_gate, grad_out = call(
        middle_kernel,
        [(blocks, BF16), (flat, BF16), (flat, BF16), ((WIDTH, WIDTH), F32), ((WIDTH, WIDTH), F32)],
        [flat, (WIDTH, WIDTH)],
        recv_mixed, normed_in, cotangent, w_gate, gain_out, w_out,
    )
    d_mixed = exchange(send_d, "col")
    d_a, d_b = call(grad_kernel, [(flat, F32), (copies, BF16)], [], recv_ab, b_all, d_mixed)
    d_b = exchange(d_b, "row")
    (send_grads,) = call(join_kernel, [(twice, BF16)], [], d_a, d_b)
    recv_grads = exchange(send_grads, "col")
    grad_pair, grad_ab = call(
        last_kernel,
        [(blocks, BF16), ((4 * WIDTH, WIDTH), F32)],
        [flat, (4 * WIDTH, WIDTH), twice],
        recv_grads, pair, pair_mask, gain_in, w_ab, w_gate, normed_in, d_gate,
    )
    both = ("row", "col")
    local = jnp.concatenate([grad_ab, grad_gate, grad_out], axis=0).reshape(RES, 1, 3 * WIDTH)
    own = jnp.sum(exchange(local, both), axis=0, keepdims=True)
    total = exchange(jnp.broadcast_to(own, local.shape), both).reshape(6 * WIDTH, WIDTH) / RES
    return (
        update,
        grad_pair,
        total[: 4 * WIDTH].T,
        total[4 * WIDTH : 5 * WIDTH],
        total[5 * WIDTH :],
    )


def solution(mesh):
    placed = (
        P("row", "col", None),
        P("row", "col"),
        P(),
        P(),
        P(),
        P(),
        P(),
        P("row", "col", None),
    )
    return jax.shard_map(
        on_device,
        mesh=mesh,
        in_specs=placed,
        out_specs=(P("row", "col", None), P("row", "col", None), P(), P(), P()),
        check_vma=False,
    )
```

```python
import jax
import jax.numpy as jnp
from jax import lax
from jax.experimental import pallas as pl
from jax.experimental.pallas import tpu as pltpu
from jax.sharding import PartitionSpec as P

F32 = jnp.float32
BF16 = jnp.bfloat16

ROWS, COLS, WIDTH = 32, 8, 128
NROW, NCOL = 8, 32
PAIRS = ROWS * COLS
GROUP = WIDTH // NCOL
RES = 256
SHARE = 3 * COLS
FINAL = 2 * COLS + SHARE
GATHER = (16, 8, 4, 2, 1)


def dot(left, right, left_dim, right_dim):
    return lax.dot_general(
        left, right, (((left_dim,), (right_dim,)), ((), ())), preferred_element_type=F32
    )


def lane_block(shape):
    return lax.broadcasted_iota(jnp.int32, shape, 1) // ROWS


def load_pairs(block, scratch):
    scratch[...] = block[...].astype(F32).reshape(PAIRS, WIDTH)
    return jnp.concatenate(
        [scratch[pl.ds(k, ROWS, stride=COLS), :] for k in range(COLS)], axis=0
    )


def store_pairs(values, scratch, block):
    for k in range(COLS):
        scratch[pl.ds(k, ROWS, stride=COLS), :] = values[k * ROWS : (k + 1) * ROWS]
    block[...] = scratch[...].reshape(ROWS, COLS, WIDTH).astype(block.dtype)


def regroup(scratch, blocks):
    return jnp.concatenate(
        [
            scratch[pl.ds(blk * WIDTH + c4, NCOL, stride=GROUP), :]
            for blk in range(blocks)
            for c4 in range(GROUP)
        ],
        axis=0,
    )


def ungroup(values, scratch, blocks):
    for blk in range(blocks):
        for c4 in range(GROUP):
            start = blk * WIDTH + c4 * NCOL
            scratch[pl.ds(blk * WIDTH + c4, NCOL, stride=GROUP), :] = values[start : start + NCOL]


def to_message(values, k):
    tile, place = k // GROUP, k % GROUP
    block = lane_block((NCOL, WIDTH))
    result = None
    for c4 in range(GROUP):
        part = values[c4 * NCOL : (c4 + 1) * NCOL, tile * WIDTH : (tile + 1) * WIDTH]
        shift = (c4 - place) * ROWS % WIDTH
        if shift:
            part = pltpu.roll(part, shift, 1)
        result = part if result is None else jnp.where(block == c4, part, result)
    return result


def from_message(pieces):
    block = lane_block((NCOL, WIDTH))
    bands = []
    for c4 in range(GROUP):
        tiles = []
        for tile in range(COLS // GROUP):
            result = None
            for place in range(GROUP):
                part = pieces[tile * GROUP + place]
                shift = (place - c4) * ROWS % WIDTH
                if shift:
                    part = pltpu.roll(part, shift, 1)
                result = part if result is None else jnp.where(block == place, part, result)
            tiles.append(result)
        bands.append(jnp.concatenate(tiles, axis=1))
    return jnp.concatenate(bands, axis=0)


def mask_rows(mask):
    flags = mask[...].astype(F32).astype(BF16)
    eye = (
        lax.broadcasted_iota(jnp.int32, (COLS, COLS), 0)
        == lax.broadcasted_iota(jnp.int32, (COLS, COLS), 1)
    ).astype(F32).astype(BF16)
    turned = dot(eye, flags, 1, 1).astype(BF16)
    spread = (
        lax.broadcasted_iota(jnp.int32, (ROWS, WIDTH), 1) % ROWS
        == lax.broadcasted_iota(jnp.int32, (ROWS, WIDTH), 0)
    ).astype(F32).astype(BF16)
    return dot(turned, spread, 1, 0)


def column_of(gain):
    row = lax.broadcasted_iota(jnp.int32, (WIDTH, WIDTH), 0)
    lane = lax.broadcasted_iota(jnp.int32, (WIDTH, WIDTH), 1)
    here = lane == (row % NCOL) * GROUP + row // NCOL
    return jnp.sum(jnp.where(here, gain, 0.0), axis=1, keepdims=True)


def layer_norm(values, axis):
    center = values - jnp.mean(values, axis=axis, keepdims=True)
    inverse = lax.rsqrt(jnp.mean(center * center, axis=axis, keepdims=True) + 1e-05)
    return center * inverse, inverse


def norm_back(grad_h, normed, inverse, axis):
    first = jnp.mean(grad_h, axis=axis, keepdims=True)
    second = jnp.mean(grad_h * normed, axis=axis, keepdims=True)
    return inverse * (grad_h - first - normed * second)


def halves(message):
    wide = message.astype(F32).reshape(NCOL, 2 * COLS, WIDTH)
    return wide[:, :COLS].reshape(PAIRS, WIDTH), wide[:, COLS:].reshape(PAIRS, WIDTH)


def project_kernel(
    pair, mask, gain, w_ab, gain_out, normed_out, wide_out, send, gain_out_kept,
    pair_here, mask_here, gain_here, w_here, rows, weights, message, sems,
):
    copies = [
        pltpu.make_async_copy(there, here, sems.at[place])
        for place, (there, here) in enumerate(
            (
                (pair, pair_here),
                (mask, mask_here),
                (gain, gain_here),
                (w_ab, w_here),
                (gain_out, gain_out_kept),
            )
        )
    ]
    for copy in copies:
        copy.start()
    for copy in copies:
        copy.wait()
    h_in, _ = layer_norm(pair_here[...].astype(F32).reshape(PAIRS, WIDTH), 1)
    rows[...] = (h_in * gain_here[...]).astype(BF16).astype(F32)
    normed = jnp.concatenate(
        [rows[pl.ds(k, ROWS, stride=COLS), :] for k in range(COLS)], axis=0
    ).astype(BF16)
    normed_out[...] = normed
    flags = mask_rows(mask_here)
    wide_out[...] = jnp.concatenate(
        [rows[i * COLS : (i + 1) * COLS] * flags[:, i : i + 1] for i in range(ROWS)], axis=1
    ).astype(BF16)
    weights[...] = w_here[...].astype(F32).T
    proj = dot(regroup(weights, 4).astype(BF16), normed, 1, 1)
    a_val = jax.nn.sigmoid(proj[0:128]) * proj[128:256]
    b_val = jax.nn.sigmoid(proj[256:384]) * proj[384:512]
    for k in range(COLS):
        flag = flags[k : k + 1]
        message[pl.ds(k, NCOL, stride=2 * COLS), :] = to_message(a_val, k) * flag
        message[pl.ds(COLS + k, NCOL, stride=2 * COLS), :] = to_message(b_val, k) * flag
    send[...] = message[...].astype(BF16)


def mix_kernel(recv, b_all, send):
    a_val = halves(recv[...])[0].astype(BF16)
    block = lane_block((ROWS, WIDTH))
    for r in range(NROW):
        full = dot(b_all[r * RES : (r + 1) * RES], a_val, 0, 0)
        own = full[0:ROWS]
        for c4 in range(1, GROUP):
            own = jnp.where(block == c4, full[c4 * ROWS : (c4 + 1) * ROWS], own)
        send[r * ROWS : (r + 1) * ROWS] = own


def middle_kernel(
    recv, normed_in, cotangent, w_gate, gain, w_out,
    update, send, d_gate_out, rows, weights,
):
    mixed = from_message([recv[pl.ds(k, NCOL, stride=COLS), :] for k in range(COLS)])
    h_out, inv_out = layer_norm(mixed, 0)
    scale = column_of(gain[...])
    normed = (h_out * scale).astype(BF16)
    weights[...] = w_out[...].astype(F32)
    w_own = regroup(weights, 1).astype(BF16)
    y_val = dot(normed, w_own, 0, 0)
    flat_in = normed_in[...]
    gate = jax.nn.sigmoid(dot(flat_in, w_gate[...], 1, 0))
    store_pairs(gate * y_val, rows, update)
    cot = load_pairs(cotangent, rows)
    d_y = (cot * gate).astype(BF16)
    d_gate = (cot * y_val * gate * (1.0 - gate)).astype(BF16)
    d_gate_out[...] = d_gate
    ungroup(dot(normed, d_y, 1, 0), weights, 1)
    grad_h = dot(w_own, d_y, 1, 1) * scale
    d_mixed = norm_back(grad_h, h_out, inv_out, 0)
    for k in range(COLS):
        rows[pl.ds(k, NCOL, stride=COLS), :] = to_message(d_mixed, k)
    sums = jnp.concatenate([dot(flat_in, d_gate, 0, 0), weights[...]], axis=0)
    both = jnp.concatenate(
        [rows[...].reshape(NCOL, COLS, WIDTH), sums.reshape(NCOL, COLS, WIDTH)], axis=1
    )
    send[...] = both.reshape(2 * PAIRS, WIDTH).astype(BF16)


def grad_kernel(recv, b_all, recv_d, d_a, d_b):
    a_val = halves(recv[...])[0].astype(BF16)
    d_mixed = halves(recv_d[...])[0]
    own = (
        lax.broadcasted_iota(jnp.int32, (WIDTH, WIDTH), 0) // ROWS
        == lane_block((WIDTH, WIDTH))
    )
    total = None
    for r in range(NROW):
        part = d_mixed[r * ROWS : (r + 1) * ROWS]
        spread = jnp.where(own, jnp.concatenate([part] * GROUP, axis=0), 0.0).astype(BF16)
        term = dot(b_all[r * RES : (r + 1) * RES], spread, 1, 0)
        total = term if total is None else total + term
        d_b[r * RES : (r + 1) * RES] = dot(a_val, spread, 1, 1).astype(BF16)
    d_a[...] = total


def in_gather_order(values, col):
    for bit in range(5):
        size = COLS << bit
        pairs = values.reshape(RES // (2 * size), 2, size, WIDTH)
        swapped = jnp.concatenate([pairs[:, 1:], pairs[:, :1]], axis=1)
        values = jnp.where((col >> bit) & 1 == 1, swapped, pairs).reshape(RES, WIDTH)
    places = [0]
    for step in GATHER:
        places += [place ^ step for place in places]
    return jnp.concatenate([values[p * COLS : (p + 1) * COLS] for p in places], axis=0)


def weight_kernel(
    col, wide_0, wide_1, w_ab, d_a, d_b, recv_d, d_b_sum, send, proj, d_proj
):
    total = d_b[0:RES].astype(F32)
    for r in range(1, NROW):
        total = total + d_b[r * RES : (r + 1) * RES].astype(F32)
    d_b_sum[...] = total
    taps = 4 * GROUP
    tall = 4 * WIDTH
    tap = lax.broadcasted_iota(jnp.int32, (tall, taps), 1)
    source = tap // GROUP * WIDTH + col[0] * GROUP + tap % GROUP
    pick = (lax.broadcasted_iota(jnp.int32, (tall, taps), 0) == source).astype(F32)
    w_own = dot(pick.astype(BF16), w_ab[...], 0, 1).astype(BF16)
    sides = (wide_0, wide_1)
    for side, wide in enumerate(sides):
        for i in range(ROWS):
            part = wide[:, i * WIDTH : (i + 1) * WIDTH]
            proj[pl.ds(side * tall + i, taps, stride=ROWS), :] = dot(w_own, part, 1, 1)
    for half, d_val in enumerate((d_a[...], total)):
        turned = in_gather_order(d_val, col[0]).T
        for side in range(2):
            start = side * tall + half * 2 * WIDTH
            sig = jax.nn.sigmoid(proj[start : start + WIDTH])
            value = proj[start + WIDTH : start + 2 * WIDTH]
            d_value = turned[:, side * WIDTH : (side + 1) * WIDTH] * sig
            d_proj[start : start + WIDTH] = d_value * value * (1.0 - sig)
            d_proj[start + WIDTH : start + 2 * WIDTH] = d_value
    sums = None
    for side, wide in enumerate(sides):
        for i in range(ROWS):
            left = d_proj[pl.ds(side * tall + i, taps, stride=ROWS), :].astype(BF16)
            term = dot(left, wide[:, i * WIDTH : (i + 1) * WIDTH], 1, 0)
            sums = term if sums is None else sums + term
    share = jnp.sum(recv_d[...].astype(F32).reshape(NCOL, 2 * COLS, WIDTH)[:, COLS:], axis=0)
    own = jnp.concatenate([sums, share], axis=0) * (1.0 / RES)
    for r in range(NROW):
        send[r * SHARE : (r + 1) * SHARE] = own


def join_kernel(d_a, d_b, sums, send):
    total = sums[0:SHARE]
    for r in range(1, NROW):
        total = total + sums[r * SHARE : (r + 1) * SHARE]
    everything = jnp.concatenate(
        [
            d_a[...].reshape(NCOL, COLS, WIDTH),
            d_b[...].reshape(NCOL, COLS, WIDTH),
            jnp.broadcast_to(total[None], (NCOL, SHARE, WIDTH)),
        ],
        axis=1,
    )
    send[...] = everything.reshape(NCOL * FINAL, WIDTH).astype(BF16)


def last_kernel(
    recv, pair, mask, gain, w_ab, w_gate, normed_in, d_gate,
    grad_pair, grad_ab, grad_gate, grad_out, rows, weights, message,
):
    values = load_pairs(pair, rows)
    h_in, inv_in = layer_norm(values, 1)
    flat_in = normed_in[...]
    weights[...] = w_ab[...].astype(F32).T
    w_own = regroup(weights, 4).astype(BF16)
    proj = dot(w_own, flat_in, 1, 1)
    flags = mask_rows(mask)
    message[...] = recv[...].astype(F32)
    grads = []
    for half in range(2):
        pieces = [
            message[pl.ds(half * COLS + k, NCOL, stride=FINAL), :] * flags[k : k + 1]
            for k in range(COLS)
        ]
        d_val = from_message(pieces)
        sig = jax.nn.sigmoid(proj[half * 256 : half * 256 + 128])
        value = proj[half * 256 + 128 : half * 256 + 256]
        d_value = d_val * sig
        grads += [d_value * value * (1.0 - sig), d_value]
    d_proj = jnp.concatenate(grads, axis=0).astype(BF16)
    d_in = dot(d_proj, w_own, 0, 0) + dot(d_gate[...], w_gate[...], 1, 1)
    store_pairs(norm_back(d_in * gain[...], h_in, inv_in, 1), rows, grad_pair)
    for blk in range(4):
        for c4 in range(GROUP):
            weights[pl.ds(blk * WIDTH + c4, NCOL, stride=GROUP), :] = message[
                pl.ds(2 * COLS + blk * GROUP + c4, NCOL, stride=FINAL), :
            ]
    grad_ab[...] = weights[...].T
    others = message[...].reshape(NCOL, FINAL, WIDTH)[:, FINAL - COLS :].reshape(PAIRS, WIDTH)
    grad_gate[...] = others[:WIDTH]
    grad_out[...] = others[WIDTH:]


def call(kernel, outs, scratch, *args, places=None):
    return pl.pallas_call(
        kernel,
        out_shape=[jax.ShapeDtypeStruct(shape, dtype) for shape, dtype in outs],
        in_specs=[
            pl.BlockSpec(memory_space=pltpu.VMEM if places is None else places[n])
            for n in range(len(args))
        ],
        scratch_shapes=scratch,
        compiler_params=pltpu.CompilerParams(vmem_limit_bytes=32 * 1024 * 1024),
    )(*args)


def exchange(values, axis):
    return lax.all_to_all(values, axis, 0, 0, tiled=True)


def beside(values, axis, held, step):
    values, held = lax.optimization_barrier((values, held))
    came = lax.ppermute(held, "col", [(col, col ^ step) for col in range(NCOL)])
    return lax.optimization_barrier((exchange(values, axis), held, came))


def on_device(pair, pair_mask, ln_in_gain, w_ab, w_gate, ln_out_gain, w_out, cotangent):
    gain_in = ln_in_gain.reshape(1, WIDTH)
    gain_out = ln_out_gain.reshape(1, WIDTH)
    col = lax.axis_index("col").astype(jnp.int32).reshape(1)
    flat = (PAIRS, WIDTH)
    twice = (2 * PAIRS, WIDTH)
    copies = (NROW * RES, WIDTH)
    blocks = (ROWS, COLS, WIDTH)
    square = (WIDTH, WIDTH)
    wide = (WIDTH, 4 * WIDTH)
    tall = (4 * WIDTH, WIDTH)
    normed_in, wide_in, send_ab, gain_out = call(
        project_kernel,
        [(flat, BF16), ((COLS, ROWS * WIDTH), BF16), (twice, BF16), ((1, WIDTH), F32)],
        [
            pltpu.VMEM(blocks, BF16),
            pltpu.VMEM((ROWS, COLS), jnp.int32),
            pltpu.VMEM((1, WIDTH), F32),
            pltpu.VMEM(wide, BF16),
            pltpu.VMEM(flat, F32),
            pltpu.VMEM(tall, F32),
            pltpu.VMEM(twice, F32),
            pltpu.SemaphoreType.DMA((5,)),
        ],
        pair, pair_mask, gain_in, w_ab, gain_out,
        places=[pltpu.HBM] * 5,
    )
    recv_ab, held, came = beside(send_ab, "col", wide_in, GATHER[0])
    held = jnp.concatenate([held, came], axis=0)
    b_own = recv_ab.reshape(NCOL, 2 * COLS, WIDTH)[:, COLS:].reshape(flat)
    copied = jnp.broadcast_to(b_own[None], (NROW,) + flat).reshape(copies)
    b_all, held, came = beside(copied, "row", held, GATHER[1])
    held = jnp.concatenate([held, came], axis=0)
    (send_mixed,) = call(mix_kernel, [(flat, F32)], [], recv_ab, b_all)
    recv_mixed, held, came = beside(send_mixed, "col", held, GATHER[2])
    held = jnp.concatenate([held, came], axis=0)
    update, send_d, d_gate = call(
        middle_kernel,
        [(blocks, BF16), (twice, BF16), (flat, BF16)],
        [pltpu.VMEM(flat, F32), pltpu.VMEM(square, F32)],
        recv_mixed, normed_in, cotangent, w_gate, gain_out, w_out,
    )
    recv_d, held, came = beside(send_d, "col", held, GATHER[3])
    held = jnp.concatenate([held, came], axis=0)
    d_a, d_b = call(grad_kernel, [(flat, F32), (copies, BF16)], [], recv_ab, b_all, recv_d)
    d_b, held, came = beside(d_b, "row", held, GATHER[4])
    d_b, sums = call(
        weight_kernel,
        [(flat, F32), ((NROW * SHARE, WIDTH), F32)],
        [pltpu.VMEM((8 * WIDTH, WIDTH), F32), pltpu.VMEM((8 * WIDTH, WIDTH), F32)],
        col, held, came, w_ab, d_a, d_b, recv_d,
        places=[pltpu.SMEM] + [pltpu.VMEM] * 6,
    )
    sums = exchange(sums, "row")
    (send_last,) = call(join_kernel, [((NCOL * FINAL, WIDTH), BF16)], [], d_a, d_b, sums)
    recv_last = exchange(send_last, "col")
    return call(
        last_kernel,
        [(blocks, BF16), (wide, F32), (square, F32), (square, F32)],
        [pltpu.VMEM(flat, F32), pltpu.VMEM(tall, F32), pltpu.VMEM((NCOL * FINAL, WIDTH), F32)],
        recv_last, pair, pair_mask, gain_in, w_ab, w_gate, normed_in, d_gate,
    ), update


def all_outputs(*args):
    (grad_pair, grad_ab, grad_gate, grad_out), update = on_device(*args)
    return update, grad_pair, grad_ab, grad_gate, grad_out


def solution(mesh):
    placed = (
        P("row", "col", None),
        P("row", "col"),
        P(),
        P(),
        P(),
        P(),
        P(),
        P("row", "col", None),
    )
    return jax.shard_map(
        all_outputs,
        mesh=mesh,
        in_specs=placed,
        out_specs=(P("row", "col", None), P("row", "col", None), P(), P(), P()),
        check_vma=False,
    )
```

```python
import jax
import jax.numpy as jnp
from jax import lax
from jax.experimental import pallas as pl
from jax.experimental.pallas import tpu as pltpu
from jax.sharding import Mesh, PartitionSpec as P

F32 = jnp.float32
BF16 = jnp.bfloat16

ROWS, COLS, WIDTH = 32, 8, 128
NROW, NLANE, NSIDE = 8, 16, 16
PAIRS = ROWS * COLS
GROUP = WIDTH // NLANE
QUAD = WIDTH // ROWS
HALF = ROWS // 2
RES = 256
TAPS = 4 * GROUP
SHARE = TAPS + 2 * WIDTH // NLANE
FINAL = 4 * COLS + SHARE
GATHER = (("z", 4), ("z", 2), ("z", 1), ("core", 1))


def dot(left, right, left_dim, right_dim):
    return lax.dot_general(
        left, right, (((left_dim,), (right_dim,)), ((), ())), preferred_element_type=F32
    )


def lane_block(shape, size=ROWS):
    return lax.broadcasted_iota(jnp.int32, shape, 1) // size


def load_pairs(block, scratch):
    scratch[...] = block[...].astype(F32).reshape(PAIRS, WIDTH)
    return jnp.concatenate(
        [scratch[pl.ds(k, ROWS, stride=COLS), :] for k in range(COLS)], axis=0
    )


def store_pairs(values, scratch, block):
    for k in range(COLS):
        scratch[pl.ds(k, ROWS, stride=COLS), :] = values[k * ROWS : (k + 1) * ROWS]
    block[...] = scratch[...].reshape(ROWS, COLS, WIDTH).astype(block.dtype)


def regroup(scratch, blocks):
    return jnp.concatenate(
        [
            scratch[pl.ds(blk * WIDTH + cc, NLANE, stride=GROUP), :]
            for blk in range(blocks)
            for cc in range(GROUP)
        ],
        axis=0,
    )


def ungroup(values, scratch):
    for cc in range(GROUP):
        scratch[pl.ds(cc, NLANE, stride=GROUP), :] = values[cc * NLANE : (cc + 1) * NLANE]


def moved(part, shift):
    shift = shift % WIDTH
    return pltpu.roll(part, shift, 1) if shift else part


def to_message(values, k, which, size):
    tile, start = k // QUAD, k % QUAD * ROWS
    first = which * QUAD
    if size == HALF:
        start, first = start + which * HALF, 0
    block = lane_block((NLANE, WIDTH), size)
    result = None
    for place in range(WIDTH // size):
        row = (first + place) * NLANE
        part = moved(values[row : row + NLANE, tile * WIDTH : (tile + 1) * WIDTH], place * size - start)
        result = part if result is None else jnp.where(block == place, part, result)
    return result


def from_message(pieces, size):
    block = lane_block((NLANE, WIDTH), size)
    bands = []
    for cc in range(GROUP):
        tiles = []
        for tile in range(COLS // QUAD):
            result = None
            for place in range(WIDTH // size):
                if size == ROWS:
                    part = pieces[tile * QUAD + place][cc // QUAD]
                    start = cc % QUAD * ROWS
                else:
                    part = pieces[tile * QUAD + place // 2][place % 2]
                    start = cc * HALF
                part = moved(part, place * size - start)
                result = part if result is None else jnp.where(block == place, part, result)
            tiles.append(result)
        bands.append(jnp.concatenate(tiles, axis=1))
    return jnp.concatenate(bands, axis=0)


def mask_rows(mask):
    flags = mask[...].astype(F32).astype(BF16)
    source = lax.broadcasted_iota(jnp.int32, (ROWS, WIDTH), 0)
    lane = lax.broadcasted_iota(jnp.int32, (ROWS, WIDTH), 1)
    return [
        dot(flags, (place == source).astype(F32).astype(BF16), 1, 0)
        for place in (lane % ROWS, lane % HALF, lane % HALF + HALF)
    ]


def column_of(gain):
    row = lax.broadcasted_iota(jnp.int32, (WIDTH, WIDTH), 0)
    lane = lax.broadcasted_iota(jnp.int32, (WIDTH, WIDTH), 1)
    here = lane == (row % NLANE) * GROUP + row // NLANE
    return jnp.sum(jnp.where(here, gain, 0.0), axis=1, keepdims=True)


def layer_norm(values, axis):
    center = values - jnp.mean(values, axis=axis, keepdims=True)
    inverse = lax.rsqrt(jnp.mean(center * center, axis=axis, keepdims=True) + 1e-05)
    return center * inverse, inverse


def norm_back(grad_h, normed, inverse, axis):
    first = jnp.mean(grad_h, axis=axis, keepdims=True)
    second = jnp.mean(grad_h * normed, axis=axis, keepdims=True)
    return inverse * (grad_h - first - normed * second)


def split_rows(message, parts):
    wide = message.astype(F32).reshape(NLANE, parts, COLS, WIDTH)
    return [wide[:, part].reshape(NLANE * COLS, WIDTH) for part in range(parts)]


def project_kernel(*refs):
    count = len(refs) - 7
    inputs, kept = refs[: count // 2], refs[count // 2 : count]
    normed_out, wide_out, send, rows, weights, message, sems = refs[count:]
    copies = [
        pltpu.make_async_copy(there, here, sems.at[place])
        for place, (there, here) in enumerate(zip(inputs, kept))
    ]
    for copy in copies:
        copy.start()
    for copy in copies:
        copy.wait()
    pair_here, mask_here, gain_here, w_here = kept[:4]
    h_in, _ = layer_norm(pair_here[...].astype(F32).reshape(PAIRS, WIDTH), 1)
    rows[...] = (h_in * gain_here[...]).astype(BF16).astype(F32)
    normed = jnp.concatenate(
        [rows[pl.ds(k, ROWS, stride=COLS), :] for k in range(COLS)], axis=0
    ).astype(BF16)
    normed_out[...] = normed
    flags, *half_flags = mask_rows(mask_here)
    wide_out[...] = jnp.concatenate(
        [rows[i * COLS : (i + 1) * COLS] * flags[:, i : i + 1] for i in range(ROWS)], axis=1
    ).astype(BF16)
    weights[...] = w_here[...].astype(F32).T
    proj = dot(regroup(weights, 4).astype(BF16), normed, 1, 1)
    a_val = jax.nn.sigmoid(proj[0:128]) * proj[128:256]
    b_val = jax.nn.sigmoid(proj[256:384]) * proj[384:512]
    for k in range(COLS):
        for part in range(2):
            message[pl.ds(part * COLS + k, NLANE, stride=4 * COLS), :] = (
                to_message(a_val, k, part, ROWS) * flags[k : k + 1]
            )
            message[pl.ds((2 + part) * COLS + k, NLANE, stride=4 * COLS), :] = (
                to_message(b_val, k, part, HALF) * half_flags[part][k : k + 1]
            )
    send[...] = message[...].astype(BF16)


def spread_kernel(recv, send):
    parts = split_rows(recv[...], 4)
    for side in range(NSIDE):
        send[side * WIDTH : (side + 1) * WIDTH] = parts[2 + side % 2].astype(BF16)


def mix_kernel(recv, recv_near, b_all, send, a_all):
    own, near = split_rows(recv[...], 4), split_rows(recv_near[...], 4)
    is_first = lax.axis_index("y") == 0
    a_val = []
    for first, second in ((own, near), (near, own)):
        a_val.append(
            jnp.concatenate(
                [jnp.where(is_first, first[h], second[h]) for h in range(2)], axis=1
            ).astype(BF16)
        )
    a_all[...] = jnp.concatenate(a_val, axis=0)
    block = lane_block((HALF, WIDTH))
    pieces = []
    for r in range(NROW):
        full = None
        for y in range(2):
            side = 2 * r + y
            term = dot(b_all[side * WIDTH : (side + 1) * WIDTH], a_val[y], 0, 0)
            full = term if full is None else full + term
        found = []
        for h in range(2):
            mixed = None
            for c4 in range(QUAD):
                row = (h * QUAD + c4) * HALF
                part = full[row : row + HALF, h * WIDTH : (h + 1) * WIDTH]
                mixed = part if mixed is None else jnp.where(block == c4, part, mixed)
            found.append(mixed)
        pieces += [found[h][core * COLS : (core + 1) * COLS] for core in range(2) for h in range(2)]
    send[...] = jnp.concatenate(pieces, axis=0).astype(BF16)


def middle_kernel(
    recv, normed_in, cotangent, w_gate, gain, w_out,
    update, send, d_gate_out, rows, weights,
):
    rows[...] = recv[...].astype(F32)
    mixed = from_message(
        [
            [rows[pl.ds(h * COLS + k, NLANE, stride=2 * COLS), :] for h in range(2)]
            for k in range(COLS)
        ],
        ROWS,
    )
    h_out, inv_out = layer_norm(mixed, 0)
    scale = column_of(gain[...])
    normed = (h_out * scale).astype(BF16)
    weights[...] = w_out[...].astype(F32)
    w_own = regroup(weights, 1).astype(BF16)
    y_val = dot(normed, w_own, 0, 0)
    flat_in = normed_in[...]
    gate = jax.nn.sigmoid(dot(flat_in, w_gate[...], 1, 0))
    store_pairs(gate * y_val, rows, update)
    cot = load_pairs(cotangent, rows)
    d_y = (cot * gate).astype(BF16)
    d_gate = (cot * y_val * gate * (1.0 - gate)).astype(BF16)
    d_gate_out[...] = d_gate
    ungroup(dot(normed, d_y, 1, 0), weights)
    grad_h = dot(w_own, d_y, 1, 1) * scale
    d_mixed = norm_back(grad_h, h_out, inv_out, 0)
    for k in range(COLS):
        for h in range(2):
            rows[pl.ds(h * COLS + k, NLANE, stride=2 * COLS), :] = to_message(d_mixed, k, h, ROWS)
    sums = jnp.concatenate([dot(flat_in, d_gate, 0, 0), weights[...]], axis=0)
    both = jnp.concatenate(
        [rows[...].reshape(NLANE, 2 * COLS, WIDTH), sums.reshape(NLANE, 2 * COLS, WIDTH)], axis=1
    )
    send[...] = both.reshape(2 * PAIRS, WIDTH).astype(BF16)


def grad_kernel(a_all, b_all, recv_d, d_a_own, d_a_near, d_b):
    d_mixed = split_rows(recv_d[...], 4)[:2]
    a_val = [a_all[y * WIDTH : (y + 1) * WIDTH] for y in range(2)]
    block = lane_block((HALF, WIDTH))
    totals = [None, None]
    for r in range(NROW):
        tiles = []
        for h in range(2):
            part = d_mixed[h][r * HALF : (r + 1) * HALF]
            nothing = jnp.zeros_like(part)
            tiles.append(
                jnp.concatenate(
                    [
                        jnp.where(block == cc % QUAD, part, nothing) if cc // QUAD == h else nothing
                        for cc in range(GROUP)
                    ],
                    axis=0,
                )
            )
        spread = jnp.concatenate(tiles, axis=1).astype(BF16)
        for y in range(2):
            side = 2 * r + y
            term = dot(b_all[side * WIDTH : (side + 1) * WIDTH], spread, 1, 0)
            totals[y] = term if totals[y] is None else totals[y] + term
            d_b[side * WIDTH : (side + 1) * WIDTH] = dot(a_val[y], spread, 1, 1).astype(BF16)
    is_first = lax.axis_index("y") == 0
    for h in range(2):
        first, second = (total[:, h * WIDTH : (h + 1) * WIDTH] for total in totals)
        d_a_own[h * WIDTH : (h + 1) * WIDTH] = jnp.where(is_first, first, second)
        d_a_near[h * WIDTH : (h + 1) * WIDTH] = jnp.where(is_first, second, first).astype(BF16)


def in_gather_order(values, lane):
    for bit in range(4):
        size = COLS << bit
        pairs = values.reshape(WIDTH // (2 * size), 2, size, WIDTH)
        swapped = jnp.concatenate([pairs[:, 1:], pairs[:, :1]], axis=1)
        values = jnp.where((lane >> bit) & 1 == 1, swapped, pairs).reshape(WIDTH, WIDTH)
    places = [0]
    for axis, step in GATHER:
        places += [place ^ (2 * step if axis == "z" else step) for place in places]
    return jnp.concatenate([values[p * COLS : (p + 1) * COLS] for p in places], axis=0)


def weight_kernel(
    wide_0, wide_1, w_ab, d_a_own, d_a_near, d_b, recv_d, d_a_sum, d_b_sum, send, proj, d_proj
):
    lane = lax.axis_index("z") * 2 + lax.axis_index("core")
    d_a = d_a_own[...] + d_a_near[...].astype(F32)
    d_a_sum[...] = d_a
    totals = []
    for y in range(2):
        total = d_b[y * WIDTH : (y + 1) * WIDTH].astype(F32)
        for r in range(1, NROW):
            side = 2 * r + y
            total = total + d_b[side * WIDTH : (side + 1) * WIDTH].astype(F32)
        totals.append(total)
    d_b_sum[...] = jnp.concatenate(totals, axis=0)
    tall = 4 * WIDTH
    tap = lax.broadcasted_iota(jnp.int32, (tall, TAPS), 1)
    source = tap // GROUP * WIDTH + lane * GROUP + tap % GROUP
    pick = (lax.broadcasted_iota(jnp.int32, (tall, TAPS), 0) == source).astype(F32)
    w_own = dot(pick.astype(BF16), w_ab[...], 0, 1)
    nothing = jnp.zeros_like(w_own)
    w_twice = jnp.concatenate(
        [jnp.concatenate([w_own, nothing], axis=1), jnp.concatenate([nothing, w_own], axis=1)],
        axis=0,
    ).astype(BF16)
    parts = []
    for i in range(0, ROWS, 2):
        lanes = slice(i * WIDTH, (i + 2) * WIDTH)
        part = jnp.concatenate([wide_0[:, lanes], wide_1[:, lanes]], axis=0)
        parts.append(part)
        values = dot(w_twice, part, 1, 1)
        for odd in range(2):
            proj[pl.ds(i + odd, TAPS, stride=ROWS), :] = values[odd * TAPS : (odd + 1) * TAPS]
    turned_a = jnp.concatenate(
        [in_gather_order(d_a[h * WIDTH : (h + 1) * WIDTH], lane).T for h in range(2)], axis=0
    )
    sides = [in_gather_order(total, lane).T for total in totals]
    turned_b = jnp.concatenate(
        [side[cc * HALF : (cc + 1) * HALF] for cc in range(GROUP) for side in sides], axis=0
    )
    for half, d_val in enumerate((turned_a, turned_b)):
        start = half * 2 * RES
        sig = jax.nn.sigmoid(proj[start : start + RES])
        value = proj[start + RES : start + 2 * RES]
        d_value = d_val * sig
        d_proj[start : start + RES] = d_value * value * (1.0 - sig)
        d_proj[start + RES : start + 2 * RES] = d_value
    sums = None
    for i in range(0, ROWS, 2):
        left = jnp.concatenate(
            [d_proj[pl.ds(i + odd, TAPS, stride=ROWS), :] for odd in range(2)], axis=0
        ).astype(BF16)
        both = dot(left, parts[i // 2], 1, 0)
        term = both[:TAPS, :WIDTH] + both[TAPS:, WIDTH:]
        sums = term if sums is None else sums + term
    others = recv_d[...].astype(F32).reshape(NLANE, 4 * COLS, WIDTH)[:, 2 * COLS :]
    own = jnp.concatenate([sums, jnp.sum(others, axis=0)], axis=0) * (1.0 / RES)
    for side in range(NSIDE):
        send[side * SHARE : (side + 1) * SHARE] = own.astype(BF16)


def join_kernel(d_a, d_b, sums, send):
    total = jnp.sum(sums[...].astype(F32).reshape(NSIDE, SHARE, WIDTH), axis=0)
    pieces = [
        half[part * WIDTH : (part + 1) * WIDTH].reshape(NLANE, COLS, WIDTH)
        for half in (d_a, d_b)
        for part in range(2)
    ]
    pieces.append(jnp.broadcast_to(total[None], (NLANE, SHARE, WIDTH)))
    send[...] = jnp.concatenate(pieces, axis=1).reshape(NLANE * FINAL, WIDTH).astype(BF16)


def last_kernel(
    recv, pair, mask, gain, w_ab, w_gate, normed_in, d_gate,
    grad_pair, grad_ab, grad_gate, grad_out, rows, weights, message,
):
    values = load_pairs(pair, rows)
    h_in, inv_in = layer_norm(values, 1)
    flat_in = normed_in[...]
    weights[...] = w_ab[...].astype(F32).T
    w_own = regroup(weights, 4).astype(BF16)
    proj = dot(w_own, flat_in, 1, 1)
    flags, *half_flags = mask_rows(mask)
    message[...] = recv[...].astype(F32)
    grads = []
    for half, size in enumerate((ROWS, HALF)):
        pieces = [
            [
                message[pl.ds((half * 2 + part) * COLS + k, NLANE, stride=FINAL), :]
                * (half_flags[part] if half else flags)[k : k + 1]
                for part in range(2)
            ]
            for k in range(COLS)
        ]
        d_val = from_message(pieces, size)
        sig = jax.nn.sigmoid(proj[half * 256 : half * 256 + 128])
        value = proj[half * 256 + 128 : half * 256 + 256]
        d_value = d_val * sig
        grads += [d_value * value * (1.0 - sig), d_value]
    d_proj = jnp.concatenate(grads, axis=0).astype(BF16)
    d_in = dot(d_proj, w_own, 0, 0) + dot(d_gate[...], w_gate[...], 1, 1)
    store_pairs(norm_back(d_in * gain[...], h_in, inv_in, 1), rows, grad_pair)
    for blk in range(4):
        for cc in range(GROUP):
            weights[pl.ds(blk * WIDTH + cc, NLANE, stride=GROUP), :] = message[
                pl.ds(4 * COLS + blk * GROUP + cc, NLANE, stride=FINAL), :
            ]
    grad_ab[...] = weights[...].T
    others = message[...].reshape(NLANE, FINAL, WIDTH)[:, 4 * COLS + TAPS :].reshape(PAIRS, WIDTH)
    grad_gate[...] = others[:WIDTH]
    grad_out[...] = others[WIDTH:]


def call(kernel, outs, scratch, *args, places=None):
    return pl.pallas_call(
        kernel,
        out_shape=[jax.ShapeDtypeStruct(shape, dtype) for shape, dtype in outs],
        in_specs=[
            pl.BlockSpec(memory_space=pltpu.VMEM if places is None else places[n])
            for n in range(len(args))
        ],
        scratch_shapes=scratch,
        compiler_params=pltpu.CompilerParams(vmem_limit_bytes=32 * 1024 * 1024),
    )(*args)


LANES = ("z", "core")
SIDES = ("row", "y")


def exchange(values, axes):
    return lax.all_to_all(values, axes, 0, 0, tiled=True)


def swap(values, axis, step):
    return lax.ppermute(values, axis, [(n, n ^ step) for n in range(lax.axis_size(axis))])


def beside(values, axes, *swaps):
    values, *held = lax.optimization_barrier((values, *(array for array, _, _ in swaps)))
    came = [swap(array, axis, step) for array, (_, axis, step) in zip(held, swaps)]
    return lax.optimization_barrier((exchange(values, axes), held, came))


def on_device(pair, pair_mask, ln_in_gain, w_ab, w_gate, ln_out_gain, w_out, cotangent):
    pair_mask = pair_mask.T
    gain_in = ln_in_gain.reshape(1, WIDTH)
    gain_out = ln_out_gain.reshape(1, WIDTH)
    flat = (PAIRS, WIDTH)
    twice = (2 * PAIRS, WIDTH)
    copies = (NSIDE * WIDTH, WIDTH)
    blocks = (ROWS, COLS, WIDTH)
    square = (WIDTH, WIDTH)
    wide = (WIDTH, 4 * WIDTH)
    tall = (4 * WIDTH, WIDTH)
    last = (NLANE * FINAL, WIDTH)
    inputs = (pair, pair_mask, gain_in, w_ab, gain_out, w_gate, w_out, cotangent)
    *inputs, normed_in, wide_in, send_ab = call(
        project_kernel,
        [(array.shape, array.dtype) for array in inputs]
        + [(flat, BF16), ((COLS, ROWS * WIDTH), BF16), (twice, BF16)],
        [
            pltpu.VMEM(flat, F32),
            pltpu.VMEM(tall, F32),
            pltpu.VMEM(twice, F32),
            pltpu.SemaphoreType.DMA((len(inputs),)),
        ],
        *(pltpu.with_memory_space_constraint(array, pltpu.HBM) for array in inputs),
        places=[pltpu.HBM] * len(inputs),
    )
    pair, pair_mask, gain_in, w_ab, gain_out, w_gate, w_out, cotangent = inputs
    recv_ab, held, came = beside(send_ab, LANES)
    held = wide_in
    (send_b,) = call(spread_kernel, [(copies, BF16)], [], recv_ab)
    b_all, (held, _), (came, recv_near) = beside(
        send_b, SIDES, (held, *GATHER[0]), (recv_ab, "y", 1)
    )
    held = jnp.concatenate([held, came], axis=0)
    send_mixed, a_all = call(
        mix_kernel, [(flat, BF16), ((2 * WIDTH, 2 * WIDTH), BF16)], [], recv_ab, recv_near, b_all
    )
    recv_mixed, held, came = beside(send_mixed, LANES, (held, *GATHER[1]))
    held = jnp.concatenate(held + came, axis=0)
    update, send_d, d_gate = call(
        middle_kernel,
        [(blocks, BF16), (twice, BF16), (flat, BF16)],
        [pltpu.VMEM(flat, F32), pltpu.VMEM(square, F32)],
        recv_mixed, normed_in, cotangent, w_gate, gain_out, w_out,
    )
    recv_d, held, came = beside(send_d, LANES, (held, *GATHER[2]))
    held = jnp.concatenate(held + came, axis=0)
    d_a_own, d_a_near, d_b = call(
        grad_kernel, [(flat, F32), (flat, BF16), (copies, BF16)], [], a_all, b_all, recv_d
    )
    d_b, (_, held), (d_a_near, came) = beside(d_b, SIDES, (d_a_near, "y", 1), (held, *GATHER[3]))
    wide_parts = [held, came]
    d_a, d_b, sums = call(
        weight_kernel,
        [(flat, F32), (flat, F32), ((NSIDE * SHARE, WIDTH), BF16)],
        [pltpu.VMEM((TAPS * ROWS, WIDTH), F32), pltpu.VMEM((TAPS * ROWS, WIDTH), F32)],
        *wide_parts, w_ab, d_a_own, d_a_near, d_b, recv_d,
    )
    sums = exchange(sums, SIDES)
    (send_last,) = call(join_kernel, [(last, BF16)], [], d_a, d_b, sums)
    recv_last = exchange(send_last, LANES)
    grad_pair, grad_ab, grad_gate, grad_out = call(
        last_kernel,
        [(blocks, BF16), (wide, F32), (square, F32), (square, F32)],
        [pltpu.VMEM(flat, F32), pltpu.VMEM(tall, F32), pltpu.VMEM(last, F32)],
        recv_last, pair, pair_mask, gain_in, w_ab, w_gate, normed_in, d_gate,
    )
    return update, grad_pair, grad_ab, grad_gate, grad_out


def solution(mesh):
    split = Mesh(mesh.devices.reshape(NROW, 8, 2, 2), ("row", "z", "y", "core"))
    cols = ("z", "y", "core")
    blocks = P("row", cols, None)
    placed = (blocks, P("row", cols), P(), P(), P(), P(), P(), blocks)
    return jax.shard_map(
        on_device,
        mesh=split,
        in_specs=placed,
        out_specs=(blocks, blocks, P(), P(), P()),
        check_vma=False,
    )
```

```python
import jax
import jax.numpy as jnp
from jax import lax
from jax.experimental import pallas as pl
from jax.experimental.pallas import tpu as pltpu
from jax.sharding import Mesh, PartitionSpec as P

F32 = jnp.float32
BF16 = jnp.bfloat16

ROWS, COLS, WIDTH = 32, 8, 128
NROW, NLANE, NSIDE = 8, 16, 16
PAIRS = ROWS * COLS
GROUP = WIDTH // NLANE
QUAD = WIDTH // ROWS
HALF = ROWS // 2
RES = 256
TAPS = 4 * GROUP
SHARE = TAPS + 2 * WIDTH // NLANE
FINAL = 4 * COLS + SHARE // 2
GATHER = (("z", 4), ("z", 2), ("z", 1), ("core", 1))


def dot(left, right, left_dim, right_dim):
    return lax.dot_general(
        left, right, (((left_dim,), (right_dim,)), ((), ())), preferred_element_type=F32
    )


def lane_block(shape, size=ROWS):
    return lax.broadcasted_iota(jnp.int32, shape, 1) // size


def load_pairs(block, scratch):
    scratch[...] = block[...].astype(F32).reshape(PAIRS, WIDTH)
    return jnp.concatenate(
        [scratch[pl.ds(k, ROWS, stride=COLS), :] for k in range(COLS)], axis=0
    )


def store_pairs(values, scratch, block):
    for k in range(COLS):
        scratch[pl.ds(k, ROWS, stride=COLS), :] = values[k * ROWS : (k + 1) * ROWS]
    block[...] = scratch[...].reshape(ROWS, COLS, WIDTH).astype(block.dtype)


def regroup(scratch, blocks):
    return jnp.concatenate(
        [
            scratch[pl.ds(blk * WIDTH + cc, NLANE, stride=GROUP), :]
            for blk in range(blocks)
            for cc in range(GROUP)
        ],
        axis=0,
    )


def ungroup(values, scratch):
    for cc in range(GROUP):
        scratch[pl.ds(cc, NLANE, stride=GROUP), :] = values[cc * NLANE : (cc + 1) * NLANE]


def moved(part, shift):
    shift = shift % WIDTH
    return pltpu.roll(part, shift, 1) if shift else part


def to_message(values, k, which, size):
    tile, start = k // QUAD, k % QUAD * ROWS
    first = which * QUAD
    if size == HALF:
        start, first = start + which * HALF, 0
    block = lane_block((NLANE, WIDTH), size)
    result = None
    for place in range(WIDTH // size):
        row = (first + place) * NLANE
        part = moved(values[row : row + NLANE, tile * WIDTH : (tile + 1) * WIDTH], place * size - start)
        result = part if result is None else jnp.where(block == place, part, result)
    return result


def from_message(pieces, size):
    block = lane_block((NLANE, WIDTH), size)
    bands = []
    for cc in range(GROUP):
        tiles = []
        for tile in range(COLS // QUAD):
            result = None
            for place in range(WIDTH // size):
                if size == ROWS:
                    part = pieces[tile * QUAD + place][cc // QUAD]
                    start = cc % QUAD * ROWS
                else:
                    part = pieces[tile * QUAD + place // 2][place % 2]
                    start = cc * HALF
                part = moved(part, place * size - start)
                result = part if result is None else jnp.where(block == place, part, result)
            tiles.append(result)
        bands.append(jnp.concatenate(tiles, axis=1))
    return jnp.concatenate(bands, axis=0)


def mask_rows(mask):
    flags = mask[...].astype(F32).astype(BF16)
    source = lax.broadcasted_iota(jnp.int32, (ROWS, WIDTH), 0)
    lane = lax.broadcasted_iota(jnp.int32, (ROWS, WIDTH), 1)
    return [
        dot(flags, (place == source).astype(F32).astype(BF16), 1, 0)
        for place in (lane % ROWS, lane % HALF, lane % HALF + HALF)
    ]


def column_of(gain):
    row = lax.broadcasted_iota(jnp.int32, (WIDTH, WIDTH), 0)
    lane = lax.broadcasted_iota(jnp.int32, (WIDTH, WIDTH), 1)
    here = lane == (row % NLANE) * GROUP + row // NLANE
    return jnp.sum(jnp.where(here, gain, 0.0), axis=1, keepdims=True)


def layer_norm(values, axis):
    center = values - jnp.mean(values, axis=axis, keepdims=True)
    inverse = lax.rsqrt(jnp.mean(center * center, axis=axis, keepdims=True) + 1e-05)
    return center * inverse, inverse


def norm_back(grad_h, normed, inverse, axis):
    first = jnp.mean(grad_h, axis=axis, keepdims=True)
    second = jnp.mean(grad_h * normed, axis=axis, keepdims=True)
    return inverse * (grad_h - first - normed * second)


def split_rows(message, parts):
    wide = message.astype(F32).reshape(NLANE, parts, COLS, WIDTH)
    return [wide[:, part].reshape(NLANE * COLS, WIDTH) for part in range(parts)]


def project_kernel(*refs):
    count = len(refs) - 7
    inputs, kept = refs[: count // 2], refs[count // 2 : count]
    normed_out, wide_out, send, rows, weights, message, sems = refs[count:]
    copies = [
        pltpu.make_async_copy(there, here, sems.at[place])
        for place, (there, here) in enumerate(zip(inputs, kept))
    ]
    for copy in copies:
        copy.start()
    for copy in copies:
        copy.wait()
    pair_here, mask_here, gain_here, w_here = kept[:4]
    h_in, _ = layer_norm(pair_here[...].astype(F32).reshape(PAIRS, WIDTH), 1)
    rows[...] = (h_in * gain_here[...]).astype(BF16).astype(F32)
    normed = jnp.concatenate(
        [rows[pl.ds(k, ROWS, stride=COLS), :] for k in range(COLS)], axis=0
    ).astype(BF16)
    normed_out[...] = normed
    flags, *half_flags = mask_rows(mask_here)
    wide_out[...] = jnp.concatenate(
        [rows[i * COLS : (i + 1) * COLS] * flags[:, i : i + 1] for i in range(ROWS)], axis=1
    ).astype(BF16)
    weights[...] = w_here[...].astype(F32).T
    proj = dot(regroup(weights, 4).astype(BF16), normed, 1, 1)
    a_val = jax.nn.sigmoid(proj[0:128]) * proj[128:256]
    b_val = jax.nn.sigmoid(proj[256:384]) * proj[384:512]
    for k in range(COLS):
        for part in range(2):
            message[pl.ds(part * COLS + k, NLANE, stride=4 * COLS), :] = (
                to_message(a_val, k, part, ROWS) * flags[k : k + 1]
            )
            message[pl.ds((2 + part) * COLS + k, NLANE, stride=4 * COLS), :] = (
                to_message(b_val, k, part, HALF) * half_flags[part][k : k + 1]
            )
    send[...] = message[...].astype(BF16)


def spread_kernel(recv, send, a_own):
    parts = split_rows(recv[...], 4)
    a_own[...] = jnp.concatenate(parts[:2], axis=1).astype(BF16)
    for side in range(NSIDE):
        send[side * WIDTH : (side + 1) * WIDTH] = parts[2 + side % 2].astype(BF16)


def mix_kernel(own, near, b_all, send, a_all):
    is_first = lax.axis_index("y") == 0
    own, near = own[...], near[...]
    a_val = [jnp.where(is_first, own, near), jnp.where(is_first, near, own)]
    a_all[...] = jnp.concatenate(a_val, axis=0)
    block = lane_block((HALF, WIDTH))
    pieces = []
    for r in range(NROW):
        full = None
        for y in range(2):
            side = 2 * r + y
            term = dot(b_all[side * WIDTH : (side + 1) * WIDTH], a_val[y], 0, 0)
            full = term if full is None else full + term
        found = []
        for h in range(2):
            mixed = None
            for c4 in range(QUAD):
                row = (h * QUAD + c4) * HALF
                part = full[row : row + HALF, h * WIDTH : (h + 1) * WIDTH]
                mixed = part if mixed is None else jnp.where(block == c4, part, mixed)
            found.append(mixed)
        pieces += [found[h][core * COLS : (core + 1) * COLS] for core in range(2) for h in range(2)]
    send[...] = jnp.concatenate(pieces, axis=0).astype(BF16)


def prepare_kernel(
    pair, w_ab, normed_in, cotangent, w_gate, gain_out, w_out,
    h_in, inv_in, w_ab_own, factors, gate, cot, scale, w_out_own, rows, weights,
):
    h_in[...], inv_in[...] = layer_norm(load_pairs(pair, rows), 1)
    flat_in = normed_in[...]
    weights[...] = w_out[...].astype(F32)
    w_out_own[...] = regroup(weights, 1).astype(BF16)
    scale[...] = column_of(gain_out[...])
    gate[...] = jax.nn.sigmoid(dot(flat_in, w_gate[...], 1, 0))
    cot[...] = load_pairs(cotangent, rows)
    for blk in range(4):
        weights[...] = w_ab[:, blk * WIDTH : (blk + 1) * WIDTH].astype(F32).T
        w_ab_own[blk * WIDTH : (blk + 1) * WIDTH] = regroup(weights, 1).astype(BF16)
    proj = dot(w_ab_own[...], flat_in, 1, 1)
    for half in range(2):
        start = half * 2 * WIDTH
        sig = jax.nn.sigmoid(proj[start : start + WIDTH])
        value = proj[start + WIDTH : start + 2 * WIDTH]
        factors[start : start + WIDTH] = value * sig * (1.0 - sig)
        factors[start + WIDTH : start + 2 * WIDTH] = sig


def middle_kernel(
    recv, normed_in, gate, cot, scale, w_out_own,
    update, send, d_gate_out, rows, weights,
):
    rows[...] = recv[...].astype(F32)
    mixed = from_message(
        [
            [rows[pl.ds(h * COLS + k, NLANE, stride=2 * COLS), :] for h in range(2)]
            for k in range(COLS)
        ],
        ROWS,
    )
    h_out, inv_out = layer_norm(mixed, 0)
    scale = scale[...]
    normed = (h_out * scale).astype(BF16)
    w_own = w_out_own[...]
    y_val = dot(normed, w_own, 0, 0)
    flat_in = normed_in[...]
    gate, cot = gate[...], cot[...]
    store_pairs(gate * y_val, rows, update)
    d_y = (cot * gate).astype(BF16)
    d_gate = (cot * y_val * gate * (1.0 - gate)).astype(BF16)
    d_gate_out[...] = d_gate
    ungroup(dot(normed, d_y, 1, 0), weights)
    grad_h = dot(w_own, d_y, 1, 1) * scale
    d_mixed = norm_back(grad_h, h_out, inv_out, 0)
    for k in range(COLS):
        for h in range(2):
            rows[pl.ds(h * COLS + k, NLANE, stride=2 * COLS), :] = to_message(d_mixed, k, h, ROWS)
    sums = jnp.concatenate([dot(flat_in, d_gate, 0, 0), weights[...]], axis=0)
    both = jnp.concatenate(
        [rows[...].reshape(NLANE, 2 * COLS, WIDTH), sums.reshape(NLANE, 2 * COLS, WIDTH)], axis=1
    )
    send[...] = both.reshape(2 * PAIRS, WIDTH).astype(BF16)


def grad_kernel(a_all, b_all, recv_d, d_a_own, d_a_near, d_b):
    d_mixed = split_rows(recv_d[...], 4)[:2]
    a_val = [a_all[y * WIDTH : (y + 1) * WIDTH] for y in range(2)]
    block = lane_block((HALF, WIDTH))
    totals = [None, None]
    for r in range(NROW):
        tiles = []
        for h in range(2):
            part = d_mixed[h][r * HALF : (r + 1) * HALF]
            nothing = jnp.zeros_like(part)
            tiles.append(
                jnp.concatenate(
                    [
                        jnp.where(block == cc % QUAD, part, nothing) if cc // QUAD == h else nothing
                        for cc in range(GROUP)
                    ],
                    axis=0,
                )
            )
        spread = jnp.concatenate(tiles, axis=1).astype(BF16)
        for y in range(2):
            side = 2 * r + y
            term = dot(b_all[side * WIDTH : (side + 1) * WIDTH], spread, 1, 0)
            totals[y] = term if totals[y] is None else totals[y] + term
            d_b[side * WIDTH : (side + 1) * WIDTH] = dot(a_val[y], spread, 1, 1).astype(BF16)
    is_first = lax.axis_index("y") == 0
    for h in range(2):
        first, second = (total[:, h * WIDTH : (h + 1) * WIDTH] for total in totals)
        d_a_own[h * WIDTH : (h + 1) * WIDTH] = jnp.where(is_first, first, second)
        d_a_near[h * WIDTH : (h + 1) * WIDTH] = jnp.where(is_first, second, first).astype(BF16)


def in_gather_order(values, lane):
    for bit in range(4):
        size = COLS << bit
        pairs = values.reshape(WIDTH // (2 * size), 2, size, WIDTH)
        swapped = jnp.concatenate([pairs[:, 1:], pairs[:, :1]], axis=1)
        values = jnp.where((lane >> bit) & 1 == 1, swapped, pairs).reshape(WIDTH, WIDTH)
    places = [0]
    for axis, step in GATHER:
        places += [place ^ (2 * step if axis == "z" else step) for place in places]
    return jnp.concatenate([values[p * COLS : (p + 1) * COLS] for p in places], axis=0)


def weight_kernel(
    wide_0, wide_1, w_ab, d_a_own, d_a_near, d_b, recv_d, d_a_sum, d_b_sum, send, proj, d_proj
):
    lane = lax.axis_index("z") * 2 + lax.axis_index("core")
    d_a = d_a_own[...] + d_a_near[...].astype(F32)
    d_a_sum[...] = d_a
    totals = []
    for y in range(2):
        total = d_b[y * WIDTH : (y + 1) * WIDTH].astype(F32)
        for r in range(1, NROW):
            side = 2 * r + y
            total = total + d_b[side * WIDTH : (side + 1) * WIDTH].astype(F32)
        totals.append(total)
    d_b_sum[...] = jnp.concatenate(totals, axis=0)
    tall = 4 * WIDTH
    tap = lax.broadcasted_iota(jnp.int32, (tall, TAPS), 1)
    source = tap // GROUP * WIDTH + lane * GROUP + tap % GROUP
    pick = (lax.broadcasted_iota(jnp.int32, (tall, TAPS), 0) == source).astype(F32)
    w_own = dot(pick.astype(BF16), w_ab[...], 0, 1)
    nothing = jnp.zeros_like(w_own)
    w_twice = jnp.concatenate(
        [jnp.concatenate([w_own, nothing], axis=1), jnp.concatenate([nothing, w_own], axis=1)],
        axis=0,
    ).astype(BF16)
    parts = []
    for i in range(0, ROWS, 2):
        lanes = slice(i * WIDTH, (i + 2) * WIDTH)
        part = jnp.concatenate([wide_0[:, lanes], wide_1[:, lanes]], axis=0)
        parts.append(part)
        values = dot(w_twice, part, 1, 1)
        for odd in range(2):
            proj[pl.ds(i + odd, TAPS, stride=ROWS), :] = values[odd * TAPS : (odd + 1) * TAPS]
    turned_a = jnp.concatenate(
        [in_gather_order(d_a[h * WIDTH : (h + 1) * WIDTH], lane).T for h in range(2)], axis=0
    )
    sides = [in_gather_order(total, lane).T for total in totals]
    turned_b = jnp.concatenate(
        [side[cc * HALF : (cc + 1) * HALF] for cc in range(GROUP) for side in sides], axis=0
    )
    for half, d_val in enumerate((turned_a, turned_b)):
        start = half * 2 * RES
        sig = jax.nn.sigmoid(proj[start : start + RES])
        value = proj[start + RES : start + 2 * RES]
        d_value = d_val * sig
        d_proj[start : start + RES] = d_value * value * (1.0 - sig)
        d_proj[start + RES : start + 2 * RES] = d_value
    sums = None
    for i in range(0, ROWS, 2):
        left = jnp.concatenate(
            [d_proj[pl.ds(i + odd, TAPS, stride=ROWS), :] for odd in range(2)], axis=0
        ).astype(BF16)
        both = dot(left, parts[i // 2], 1, 0)
        term = both[:TAPS, :WIDTH] + both[TAPS:, WIDTH:]
        sums = term if sums is None else sums + term
    others = recv_d[...].astype(F32).reshape(NLANE, 4 * COLS, WIDTH)[:, 2 * COLS :]
    own = jnp.concatenate([sums, jnp.sum(others, axis=0)], axis=0) * (1.0 / RES)
    for side in range(NSIDE):
        send[side * SHARE : (side + 1) * SHARE] = own.astype(BF16)


def join_kernel(d_a, d_b, sums, send):
    total = jnp.sum(sums[...].astype(F32).reshape(NSIDE, SHARE, WIDTH), axis=0)
    pieces = [
        half[part * WIDTH : (part + 1) * WIDTH].reshape(NLANE, COLS, WIDTH)
        for half in (d_a, d_b)
        for part in range(2)
    ]
    shares = jnp.broadcast_to(
        total.reshape(1, 2, SHARE // 2, WIDTH), (NLANE // 2, 2, SHARE // 2, WIDTH)
    )
    pieces.append(shares.reshape(NLANE, SHARE // 2, WIDTH))
    send[...] = jnp.concatenate(pieces, axis=1).reshape(NLANE * FINAL, WIDTH).astype(BF16)


def last_kernel(
    recv, mask, gain, w_gate, d_gate, h_in, inv_in, w_ab_own, factors,
    grad_pair, rows, message,
):
    w_own = w_ab_own[...]
    flags, *half_flags = mask_rows(mask)
    message[...] = recv[...].astype(F32)
    grads = []
    for half, size in enumerate((ROWS, HALF)):
        pieces = [
            [
                message[pl.ds((half * 2 + part) * COLS + k, NLANE, stride=FINAL), :]
                * (half_flags[part] if half else flags)[k : k + 1]
                for part in range(2)
            ]
            for k in range(COLS)
        ]
        d_val = from_message(pieces, size)
        start = half * 2 * WIDTH
        grads += [
            d_val * factors[start : start + WIDTH],
            d_val * factors[start + WIDTH : start + 2 * WIDTH],
        ]
    d_proj = jnp.concatenate(grads, axis=0).astype(BF16)
    d_in = dot(d_proj, w_own, 0, 0) + dot(d_gate[...], w_gate[...], 1, 1)
    store_pairs(norm_back(d_in * gain[...], h_in[...], inv_in[...], 1), rows, grad_pair)


def sums_kernel(recv, recv_near, grad_ab, grad_gate, grad_out, weights, message):
    own, near = (
        part[...].astype(F32).reshape(NLANE, FINAL, WIDTH)[:, 4 * COLS :]
        for part in (recv, recv_near)
    )
    is_first = lax.axis_index("core") == 0
    both = [jnp.where(is_first, own, near), jnp.where(is_first, near, own)]
    both = jnp.concatenate(both, axis=1)
    message[...] = both.reshape(NLANE * SHARE, WIDTH)
    for blk in range(4):
        for cc in range(GROUP):
            weights[pl.ds(blk * WIDTH + cc, NLANE, stride=GROUP), :] = message[
                pl.ds(blk * GROUP + cc, NLANE, stride=SHARE), :
            ]
    grad_ab[...] = weights[...].T
    others = both[:, TAPS:].reshape(PAIRS, WIDTH)
    grad_gate[...] = others[:WIDTH]
    grad_out[...] = others[WIDTH:]


def call(kernel, outs, scratch, *args, places=None, cost=None):
    return pl.pallas_call(
        kernel,
        out_shape=[jax.ShapeDtypeStruct(shape, dtype) for shape, dtype in outs],
        in_specs=[
            pl.BlockSpec(memory_space=pltpu.VMEM if places is None else places[n])
            for n in range(len(args))
        ],
        scratch_shapes=scratch,
        compiler_params=pltpu.CompilerParams(vmem_limit_bytes=32 * 1024 * 1024),
        cost_estimate=cost,
    )(*args)


LANES = ("z", "core")
SIDES = ("row", "y")


def exchange(values, axes):
    return lax.all_to_all(values, axes, 0, 0, tiled=True)


def swap(values, axis, step):
    return lax.ppermute(values, axis, [(n, n ^ step) for n in range(lax.axis_size(axis))])


def beside(values, axes, *swaps):
    held = [array for array, _, _ in swaps]
    came = [swap(array, axis, step) for array, (_, axis, step) in zip(held, swaps)]
    return lax.optimization_barrier((exchange(values, axes), held, came))


def on_device(pair, pair_mask, ln_in_gain, w_ab, w_gate, ln_out_gain, w_out, cotangent):
    pair_mask = pair_mask.T
    gain_in = ln_in_gain.reshape(1, WIDTH)
    gain_out = ln_out_gain.reshape(1, WIDTH)
    flat = (PAIRS, WIDTH)
    twice = (2 * PAIRS, WIDTH)
    copies = (NSIDE * WIDTH, WIDTH)
    blocks = (ROWS, COLS, WIDTH)
    square = (WIDTH, WIDTH)
    wide = (WIDTH, 4 * WIDTH)
    tall = (4 * WIDTH, WIDTH)
    last = (NLANE * FINAL, WIDTH)
    inputs = (pair, pair_mask, gain_in, w_ab, gain_out, w_gate, w_out, cotangent)
    *inputs, normed_in, wide_in, send_ab = call(
        project_kernel,
        [(array.shape, array.dtype) for array in inputs]
        + [(flat, BF16), ((COLS, ROWS * WIDTH), BF16), (twice, BF16)],
        [
            pltpu.VMEM(flat, F32),
            pltpu.VMEM(tall, F32),
            pltpu.VMEM(twice, F32),
            pltpu.SemaphoreType.DMA((len(inputs),)),
        ],
        *(pltpu.with_memory_space_constraint(array, pltpu.HBM) for array in inputs),
        places=[pltpu.HBM] * len(inputs),
    )
    pair, pair_mask, gain_in, w_ab, gain_out, w_gate, w_out, cotangent = inputs
    recv_ab, held, came = beside(send_ab, LANES)
    recv_ab, held = lax.optimization_barrier((recv_ab, wide_in))
    send_b, a_own = call(spread_kernel, [(copies, BF16), ((WIDTH, 2 * WIDTH), BF16)], [], recv_ab)
    send_b, held, a_own, normed_in = lax.optimization_barrier((send_b, held, a_own, normed_in))
    prepared = call(
        prepare_kernel,
        [
            (flat, F32), ((PAIRS, 1), F32), (tall, BF16), ((4 * WIDTH, PAIRS), F32),
            (flat, F32), (flat, F32), ((WIDTH, 1), F32), (square, BF16),
        ],
        [pltpu.VMEM(flat, F32), pltpu.VMEM(square, F32)],
        pair, w_ab, normed_in, cotangent, w_gate, gain_out, w_out,
        cost=pl.CostEstimate(flops=150_000_000, bytes_accessed=3000000, transcendentals=200_000),
    )
    came, a_near = swap(held, *GATHER[0]), swap(a_own, "y", 1)
    b_all, held, came, a_own, a_near, prepared = lax.optimization_barrier(
        (exchange(send_b, SIDES), held, came, a_own, a_near, prepared)
    )
    h_in, inv_in, w_ab_own, factors, gate, cot, scale, w_out_own = prepared
    held = jnp.concatenate([held, came], axis=0)
    send_mixed, a_all = call(
        mix_kernel, [(flat, BF16), ((2 * WIDTH, 2 * WIDTH), BF16)], [], a_own, a_near, b_all
    )
    recv_mixed, held, came = beside(send_mixed, LANES, (held, *GATHER[1]))
    held = jnp.concatenate(held + came, axis=0)
    update, send_d, d_gate = call(
        middle_kernel,
        [(blocks, BF16), (twice, BF16), (flat, BF16)],
        [pltpu.VMEM(flat, F32), pltpu.VMEM(square, F32)],
        recv_mixed, normed_in, gate, cot, scale, w_out_own,
    )
    recv_d, held, came = beside(send_d, LANES, (held, *GATHER[2]))
    held = jnp.concatenate(held + came, axis=0)
    d_a_own, d_a_near, d_b = call(
        grad_kernel, [(flat, F32), (flat, BF16), (copies, BF16)], [], a_all, b_all, recv_d
    )
    d_b, (_, held), (d_a_near, came) = beside(d_b, SIDES, (d_a_near, "y", 1), (held, *GATHER[3]))
    wide_parts = [held, came]
    d_a, d_b, sums = call(
        weight_kernel,
        [(flat, F32), (flat, F32), ((NSIDE * SHARE, WIDTH), BF16)],
        [pltpu.VMEM((TAPS * ROWS, WIDTH), F32), pltpu.VMEM((TAPS * ROWS, WIDTH), F32)],
        *wide_parts, w_ab, d_a_own, d_a_near, d_b, recv_d,
    )
    sums = exchange(sums, SIDES)
    (send_last,) = call(join_kernel, [(last, BF16)], [], d_a, d_b, sums)
    recv_last = exchange(send_last, LANES)
    recv_near = swap(recv_last, "core", 1)
    (grad_pair,) = call(
        last_kernel,
        [(blocks, BF16)],
        [pltpu.VMEM(flat, F32), pltpu.VMEM(last, F32)],
        recv_last, pair_mask, gain_in, w_gate, d_gate, h_in, inv_in, w_ab_own, factors,
    )
    recv_near, grad_pair = lax.optimization_barrier((recv_near, grad_pair))
    grad_ab, grad_gate, grad_out = call(
        sums_kernel,
        [(wide, F32), (square, F32), (square, F32)],
        [pltpu.VMEM(tall, F32), pltpu.VMEM((NLANE * SHARE, WIDTH), F32)],
        recv_last, recv_near,
    )
    return update, grad_pair, grad_ab, grad_gate, grad_out


def solution(mesh):
    split = Mesh(mesh.devices.reshape(NROW, 8, 2, 2), ("row", "z", "y", "core"))
    cols = ("z", "y", "core")
    blocks = P("row", cols, None)
    placed = (blocks, P("row", cols), P(), P(), P(), P(), P(), blocks)
    return jax.shard_map(
        on_device,
        mesh=split,
        in_specs=placed,
        out_specs=(blocks, blocks, P(), P(), P()),
        check_vma=False,
    )
```

```python
import jax
import jax.numpy as jnp
from jax import lax
from jax.experimental import pallas as pl
from jax.experimental.pallas import tpu as pltpu
from jax.sharding import Mesh, PartitionSpec as P

F32 = jnp.float32
BF16 = jnp.bfloat16

ROWS, COLS, WIDTH = 32, 8, 128
NROW, NLANE, NSIDE = 8, 16, 16
PAIRS = ROWS * COLS
GROUP = WIDTH // NLANE
QUAD = WIDTH // ROWS
HALF = ROWS // 2
RES = 256
TAPS = 4 * GROUP
SHARE = TAPS + 2 * WIDTH // NLANE
FINAL = 4 * COLS + SHARE // 2
GATHER = (("z", 4), ("z", 2), ("core", 1), ("z", 1))


def dot(left, right, left_dim, right_dim):
    return lax.dot_general(
        left, right, (((left_dim,), (right_dim,)), ((), ())), preferred_element_type=F32
    )


def lane_block(shape, size=ROWS):
    return lax.broadcasted_iota(jnp.int32, shape, 1) // size


def load_pairs(block, scratch):
    scratch[...] = block[...].astype(F32).reshape(PAIRS, WIDTH)
    return jnp.concatenate(
        [scratch[pl.ds(k, ROWS, stride=COLS), :] for k in range(COLS)], axis=0
    )


def store_pairs(values, scratch, block):
    for k in range(COLS):
        scratch[pl.ds(k, ROWS, stride=COLS), :] = values[k * ROWS : (k + 1) * ROWS]
    block[...] = scratch[...].reshape(ROWS, COLS, WIDTH).astype(block.dtype)


def regroup(scratch, blocks):
    return jnp.concatenate(
        [
            scratch[pl.ds(blk * WIDTH + cc, NLANE, stride=GROUP), :]
            for blk in range(blocks)
            for cc in range(GROUP)
        ],
        axis=0,
    )


def ungroup(values, scratch):
    for cc in range(GROUP):
        scratch[pl.ds(cc, NLANE, stride=GROUP), :] = values[cc * NLANE : (cc + 1) * NLANE]


def moved(part, shift):
    shift = shift % WIDTH
    return pltpu.roll(part, shift, 1) if shift else part


def to_message(values, k, which, size):
    tile, start = k // QUAD, k % QUAD * ROWS
    first = which * QUAD
    if size == HALF:
        start, first = start + which * HALF, 0
    block = lane_block((NLANE, WIDTH), size)
    result = None
    for place in range(WIDTH // size):
        row = (first + place) * NLANE
        part = moved(values[row : row + NLANE, tile * WIDTH : (tile + 1) * WIDTH], place * size - start)
        result = part if result is None else jnp.where(block == place, part, result)
    return result


def from_message(pieces, size):
    block = lane_block((NLANE, WIDTH), size)
    bands = []
    for cc in range(GROUP):
        tiles = []
        for tile in range(COLS // QUAD):
            result = None
            for place in range(WIDTH // size):
                if size == ROWS:
                    part = pieces[tile * QUAD + place][cc // QUAD]
                    start = cc % QUAD * ROWS
                else:
                    part = pieces[tile * QUAD + place // 2][place % 2]
                    start = cc * HALF
                part = moved(part, place * size - start)
                result = part if result is None else jnp.where(block == place, part, result)
            tiles.append(result)
        bands.append(jnp.concatenate(tiles, axis=1))
    return jnp.concatenate(bands, axis=0)


def mask_rows(mask):
    flags = mask[...].astype(F32).astype(BF16)
    source = lax.broadcasted_iota(jnp.int32, (ROWS, WIDTH), 0)
    lane = lax.broadcasted_iota(jnp.int32, (ROWS, WIDTH), 1)
    return [
        dot(flags, (place == source).astype(F32).astype(BF16), 1, 0)
        for place in (lane % ROWS, lane % HALF, lane % HALF + HALF)
    ]


def column_of(gain):
    row = lax.broadcasted_iota(jnp.int32, (WIDTH, WIDTH), 0)
    lane = lax.broadcasted_iota(jnp.int32, (WIDTH, WIDTH), 1)
    here = lane == (row % NLANE) * GROUP + row // NLANE
    return jnp.sum(jnp.where(here, gain, 0.0), axis=1, keepdims=True)


def layer_norm(values, axis):
    center = values - jnp.mean(values, axis=axis, keepdims=True)
    inverse = lax.rsqrt(jnp.mean(center * center, axis=axis, keepdims=True) + 1e-05)
    return center * inverse, inverse


def norm_back(grad_h, normed, inverse, axis):
    first = jnp.mean(grad_h, axis=axis, keepdims=True)
    second = jnp.mean(grad_h * normed, axis=axis, keepdims=True)
    return inverse * (grad_h - first - normed * second)


def split_rows(message, parts):
    wide = message.astype(F32).reshape(NLANE, parts, COLS, WIDTH)
    return [wide[:, part].reshape(NLANE * COLS, WIDTH) for part in range(parts)]


def project_kernel(*refs):
    count = len(refs) - 7
    inputs, kept = refs[: count // 2], refs[count // 2 : count]
    normed_out, wide_out, send, rows, weights, message, sems = refs[count:]
    copies = [
        pltpu.make_async_copy(there, here, sems.at[place])
        for place, (there, here) in enumerate(zip(inputs, kept))
    ]
    for copy in copies:
        copy.start()
    for copy in copies:
        copy.wait()
    pair_here, mask_here, gain_here, w_here = kept[:4]
    h_in, _ = layer_norm(pair_here[...].astype(F32).reshape(PAIRS, WIDTH), 1)
    rows[...] = (h_in * gain_here[...]).astype(BF16).astype(F32)
    normed = jnp.concatenate(
        [rows[pl.ds(k, ROWS, stride=COLS), :] for k in range(COLS)], axis=0
    ).astype(BF16)
    normed_out[...] = normed
    flags, *half_flags = mask_rows(mask_here)
    wide_out[...] = jnp.concatenate(
        [rows[i * COLS : (i + 1) * COLS] * flags[:, i : i + 1] for i in range(ROWS)], axis=1
    ).astype(BF16)
    weights[...] = w_here[...].astype(F32).T
    proj = dot(regroup(weights, 4).astype(BF16), normed, 1, 1)
    a_val = jax.nn.sigmoid(proj[0:128]) * proj[128:256]
    b_val = jax.nn.sigmoid(proj[256:384]) * proj[384:512]
    for k in range(COLS):
        for part in range(2):
            message[pl.ds(part * COLS + k, NLANE, stride=4 * COLS), :] = (
                to_message(a_val, k, part, ROWS) * flags[k : k + 1]
            )
            message[pl.ds((2 + part) * COLS + k, NLANE, stride=4 * COLS), :] = (
                to_message(b_val, k, part, HALF) * half_flags[part][k : k + 1]
            )
    send[...] = message[...].astype(BF16)


def spread_kernel(recv, send, a_own):
    parts = split_rows(recv[...], 4)
    a_own[...] = jnp.concatenate(parts[:2], axis=1).astype(BF16)
    for side in range(NSIDE):
        send[side * WIDTH : (side + 1) * WIDTH] = parts[2 + side % 2].astype(BF16)


def mix_kernel(own, near, b_all, send, a_all):
    is_first = lax.axis_index("y") == 0
    own, near = own[...], near[...]
    a_val = [jnp.where(is_first, own, near), jnp.where(is_first, near, own)]
    a_all[...] = jnp.concatenate(a_val, axis=0)
    block = lane_block((HALF, WIDTH))
    pieces = []
    for r in range(NROW):
        full = None
        for y in range(2):
            side = 2 * r + y
            term = dot(b_all[side * WIDTH : (side + 1) * WIDTH], a_val[y], 0, 0)
            full = term if full is None else full + term
        found = []
        for h in range(2):
            mixed = None
            for c4 in range(QUAD):
                row = (h * QUAD + c4) * HALF
                part = full[row : row + HALF, h * WIDTH : (h + 1) * WIDTH]
                mixed = part if mixed is None else jnp.where(block == c4, part, mixed)
            found.append(mixed)
        pieces += [found[h][core * COLS : (core + 1) * COLS] for core in range(2) for h in range(2)]
    send[...] = jnp.concatenate(pieces, axis=0).astype(BF16)


def prepare_kernel(
    pair, w_ab, normed_in, cotangent, w_gate, gain_out, w_out,
    h_in, inv_in, w_ab_own, factors, gate, cot, scale, w_out_own, rows, weights,
):
    h_in[...], inv_in[...] = layer_norm(load_pairs(pair, rows), 1)
    flat_in = normed_in[...]
    weights[...] = w_out[...].astype(F32)
    w_out_own[...] = regroup(weights, 1).astype(BF16)
    scale[...] = column_of(gain_out[...])
    gate[...] = jax.nn.sigmoid(dot(flat_in, w_gate[...], 1, 0))
    cot[...] = load_pairs(cotangent, rows)
    for blk in range(4):
        weights[...] = w_ab[:, blk * WIDTH : (blk + 1) * WIDTH].astype(F32).T
        w_ab_own[blk * WIDTH : (blk + 1) * WIDTH] = regroup(weights, 1).astype(BF16)
    proj = dot(w_ab_own[...], flat_in, 1, 1)
    for half in range(2):
        start = half * 2 * WIDTH
        sig = jax.nn.sigmoid(proj[start : start + WIDTH])
        value = proj[start + WIDTH : start + 2 * WIDTH]
        factors[start : start + WIDTH] = value * sig * (1.0 - sig)
        factors[start + WIDTH : start + 2 * WIDTH] = sig


def middle_kernel(
    recv, normed_in, gate, cot, scale, w_out_own,
    update, send, d_gate_out, rows, weights,
):
    rows[...] = recv[...].astype(F32)
    mixed = from_message(
        [
            [rows[pl.ds(h * COLS + k, NLANE, stride=2 * COLS), :] for h in range(2)]
            for k in range(COLS)
        ],
        ROWS,
    )
    h_out, inv_out = layer_norm(mixed, 0)
    scale = scale[...]
    normed = (h_out * scale).astype(BF16)
    w_own = w_out_own[...]
    y_val = dot(normed, w_own, 0, 0)
    flat_in = normed_in[...]
    gate, cot = gate[...], cot[...]
    store_pairs(gate * y_val, rows, update)
    d_y = (cot * gate).astype(BF16)
    d_gate = (cot * y_val * gate * (1.0 - gate)).astype(BF16)
    d_gate_out[...] = d_gate
    ungroup(dot(normed, d_y, 1, 0), weights)
    grad_h = dot(w_own, d_y, 1, 1) * scale
    d_mixed = norm_back(grad_h, h_out, inv_out, 0)
    for k in range(COLS):
        for h in range(2):
            rows[pl.ds(h * COLS + k, NLANE, stride=2 * COLS), :] = to_message(d_mixed, k, h, ROWS)
    sums = jnp.concatenate([dot(flat_in, d_gate, 0, 0), weights[...]], axis=0)
    both = jnp.concatenate(
        [rows[...].reshape(NLANE, 2 * COLS, WIDTH), sums.reshape(NLANE, 2 * COLS, WIDTH)], axis=1
    )
    send[...] = both.reshape(2 * PAIRS, WIDTH).astype(BF16)


def grad_kernel(a_all, b_all, recv_d, d_a_own, d_a_near, d_b):
    d_mixed = split_rows(recv_d[...], 4)[:2]
    a_val = [a_all[y * WIDTH : (y + 1) * WIDTH] for y in range(2)]
    block = lane_block((HALF, WIDTH))
    totals = [None, None]
    for r in range(NROW):
        tiles = []
        for h in range(2):
            part = d_mixed[h][r * HALF : (r + 1) * HALF]
            nothing = jnp.zeros_like(part)
            tiles.append(
                jnp.concatenate(
                    [
                        jnp.where(block == cc % QUAD, part, nothing) if cc // QUAD == h else nothing
                        for cc in range(GROUP)
                    ],
                    axis=0,
                )
            )
        spread = jnp.concatenate(tiles, axis=1).astype(BF16)
        for y in range(2):
            side = 2 * r + y
            term = dot(b_all[side * WIDTH : (side + 1) * WIDTH], spread, 1, 0)
            totals[y] = term if totals[y] is None else totals[y] + term
            d_b[side * WIDTH : (side + 1) * WIDTH] = dot(a_val[y], spread, 1, 1).astype(BF16)
    is_first = lax.axis_index("y") == 0
    for h in range(2):
        first, second = (total[:, h * WIDTH : (h + 1) * WIDTH] for total in totals)
        d_a_own[h * WIDTH : (h + 1) * WIDTH] = jnp.where(is_first, first, second)
        d_a_near[h * WIDTH : (h + 1) * WIDTH] = jnp.where(is_first, second, first).astype(BF16)


def in_gather_order(values, lane):
    for bit in range(4):
        size = COLS << bit
        pairs = values.reshape(WIDTH // (2 * size), 2, size, WIDTH)
        swapped = jnp.concatenate([pairs[:, 1:], pairs[:, :1]], axis=1)
        values = jnp.where((lane >> bit) & 1 == 1, swapped, pairs).reshape(WIDTH, WIDTH)
    places = [0]
    for axis, step in GATHER:
        places += [place ^ (2 * step if axis == "z" else step) for place in places]
    return jnp.concatenate([values[p * COLS : (p + 1) * COLS] for p in places], axis=0)


def weight_kernel(
    wide_0, wide_1, w_ab, d_a_own, d_a_near, d_b, recv_d, d_a_sum, d_b_sum, send, proj, d_proj
):
    lane = lax.axis_index("z") * 2 + lax.axis_index("core")
    d_a = d_a_own[...] + d_a_near[...].astype(F32)
    d_a_sum[...] = d_a
    totals = []
    for y in range(2):
        total = d_b[y * WIDTH : (y + 1) * WIDTH].astype(F32)
        for r in range(1, NROW):
            side = 2 * r + y
            total = total + d_b[side * WIDTH : (side + 1) * WIDTH].astype(F32)
        totals.append(total)
    d_b_sum[...] = jnp.concatenate(totals, axis=0)
    tall = 4 * WIDTH
    tap = lax.broadcasted_iota(jnp.int32, (tall, TAPS), 1)
    source = tap // GROUP * WIDTH + lane * GROUP + tap % GROUP
    pick = (lax.broadcasted_iota(jnp.int32, (tall, TAPS), 0) == source).astype(F32)
    w_own = dot(pick.astype(BF16), w_ab[...], 0, 1)
    nothing = jnp.zeros_like(w_own)
    w_twice = jnp.concatenate(
        [jnp.concatenate([w_own, nothing], axis=1), jnp.concatenate([nothing, w_own], axis=1)],
        axis=0,
    ).astype(BF16)
    parts = []
    for i in range(0, ROWS, 2):
        lanes = slice(i * WIDTH, (i + 2) * WIDTH)
        part = jnp.concatenate([wide_0[:, lanes], wide_1[:, lanes]], axis=0)
        parts.append(part)
        values = dot(w_twice, part, 1, 1)
        for odd in range(2):
            proj[pl.ds(i + odd, TAPS, stride=ROWS), :] = values[odd * TAPS : (odd + 1) * TAPS]
    turned_a = jnp.concatenate(
        [in_gather_order(d_a[h * WIDTH : (h + 1) * WIDTH], lane).T for h in range(2)], axis=0
    )
    sides = [in_gather_order(total, lane).T for total in totals]
    turned_b = jnp.concatenate(
        [side[cc * HALF : (cc + 1) * HALF] for cc in range(GROUP) for side in sides], axis=0
    )
    for half, d_val in enumerate((turned_a, turned_b)):
        start = half * 2 * RES
        sig = jax.nn.sigmoid(proj[start : start + RES])
        value = proj[start + RES : start + 2 * RES]
        d_value = d_val * sig
        d_proj[start : start + RES] = d_value * value * (1.0 - sig)
        d_proj[start + RES : start + 2 * RES] = d_value
    sums = None
    for i in range(0, ROWS, 2):
        left = jnp.concatenate(
            [d_proj[pl.ds(i + odd, TAPS, stride=ROWS), :] for odd in range(2)], axis=0
        ).astype(BF16)
        both = dot(left, parts[i // 2], 1, 0)
        term = both[:TAPS, :WIDTH] + both[TAPS:, WIDTH:]
        sums = term if sums is None else sums + term
    others = recv_d[...].astype(F32).reshape(NLANE, 4 * COLS, WIDTH)[:, 2 * COLS :]
    own = jnp.concatenate([sums, jnp.sum(others, axis=0)], axis=0) * (1.0 / RES)
    for side in range(NSIDE):
        send[side * SHARE : (side + 1) * SHARE] = own.astype(BF16)


def join_kernel(d_a, d_b, sums, send):
    total = jnp.sum(sums[...].astype(F32).reshape(NSIDE, SHARE, WIDTH), axis=0)
    pieces = [
        half[part * WIDTH : (part + 1) * WIDTH].reshape(NLANE, COLS, WIDTH)
        for half in (d_a, d_b)
        for part in range(2)
    ]
    shares = jnp.broadcast_to(
        total.reshape(1, 2, SHARE // 2, WIDTH), (NLANE // 2, 2, SHARE // 2, WIDTH)
    )
    pieces.append(shares.reshape(NLANE, SHARE // 2, WIDTH))
    send[...] = jnp.concatenate(pieces, axis=1).reshape(NLANE * FINAL, WIDTH).astype(BF16)


def last_kernel(
    recv, mask, gain, w_gate, d_gate, h_in, inv_in, w_ab_own, factors,
    grad_pair, rows, message,
):
    w_own = w_ab_own[...]
    flags, *half_flags = mask_rows(mask)
    message[...] = recv[...].astype(F32)
    grads = []
    for half, size in enumerate((ROWS, HALF)):
        pieces = [
            [
                message[pl.ds((half * 2 + part) * COLS + k, NLANE, stride=FINAL), :]
                * (half_flags[part] if half else flags)[k : k + 1]
                for part in range(2)
            ]
            for k in range(COLS)
        ]
        d_val = from_message(pieces, size)
        start = half * 2 * WIDTH
        grads += [
            d_val * factors[start : start + WIDTH],
            d_val * factors[start + WIDTH : start + 2 * WIDTH],
        ]
    d_proj = jnp.concatenate(grads, axis=0).astype(BF16)
    d_in = dot(d_proj, w_own, 0, 0) + dot(d_gate[...], w_gate[...], 1, 1)
    store_pairs(norm_back(d_in * gain[...], h_in[...], inv_in[...], 1), rows, grad_pair)


def sums_kernel(recv, recv_near, grad_ab, grad_gate, grad_out, weights, message):
    own, near = (
        part[...].astype(F32).reshape(NLANE, FINAL, WIDTH)[:, 4 * COLS :]
        for part in (recv, recv_near)
    )
    is_first = lax.axis_index("core") == 0
    both = [jnp.where(is_first, own, near), jnp.where(is_first, near, own)]
    both = jnp.concatenate(both, axis=1)
    message[...] = both.reshape(NLANE * SHARE, WIDTH)
    for blk in range(4):
        for cc in range(GROUP):
            weights[pl.ds(blk * WIDTH + cc, NLANE, stride=GROUP), :] = message[
                pl.ds(blk * GROUP + cc, NLANE, stride=SHARE), :
            ]
    grad_ab[...] = weights[...].T
    others = both[:, TAPS:].reshape(PAIRS, WIDTH)
    grad_gate[...] = others[:WIDTH]
    grad_out[...] = others[WIDTH:]


def call(kernel, outs, scratch, *args, places=None, cost=None):
    return pl.pallas_call(
        kernel,
        out_shape=[jax.ShapeDtypeStruct(shape, dtype) for shape, dtype in outs],
        in_specs=[
            pl.BlockSpec(memory_space=pltpu.VMEM if places is None else places[n])
            for n in range(len(args))
        ],
        scratch_shapes=scratch,
        compiler_params=pltpu.CompilerParams(vmem_limit_bytes=32 * 1024 * 1024),
        cost_estimate=cost,
    )(*args)


LANES = ("z", "core")
SIDES = ("row", "y")


def exchange(values, axes):
    return lax.all_to_all(values, axes, 0, 0, tiled=True)


def swap(values, axis, step):
    return lax.ppermute(values, axis, [(n, n ^ step) for n in range(lax.axis_size(axis))])


def beside(values, axes, *swaps):
    held = [array for array, _, _ in swaps]
    came = [swap(array, axis, step) for array, (_, axis, step) in zip(held, swaps)]
    return lax.optimization_barrier((exchange(values, axes), held, came))


def on_device(pair, pair_mask, ln_in_gain, w_ab, w_gate, ln_out_gain, w_out, cotangent):
    pair_mask = pair_mask.T
    gain_in = ln_in_gain.reshape(1, WIDTH)
    gain_out = ln_out_gain.reshape(1, WIDTH)
    flat = (PAIRS, WIDTH)
    twice = (2 * PAIRS, WIDTH)
    copies = (NSIDE * WIDTH, WIDTH)
    blocks = (ROWS, COLS, WIDTH)
    square = (WIDTH, WIDTH)
    wide = (WIDTH, 4 * WIDTH)
    tall = (4 * WIDTH, WIDTH)
    last = (NLANE * FINAL, WIDTH)
    inputs = (pair, pair_mask, gain_in, w_ab, gain_out, w_gate, w_out, cotangent)
    *inputs, normed_in, wide_in, send_ab = call(
        project_kernel,
        [(array.shape, array.dtype) for array in inputs]
        + [(flat, BF16), ((COLS, ROWS * WIDTH), BF16), (twice, BF16)],
        [
            pltpu.VMEM(flat, F32),
            pltpu.VMEM(tall, F32),
            pltpu.VMEM(twice, F32),
            pltpu.SemaphoreType.DMA((len(inputs),)),
        ],
        *(pltpu.with_memory_space_constraint(array, pltpu.HBM) for array in inputs),
        places=[pltpu.HBM] * len(inputs),
    )
    pair, pair_mask, gain_in, w_ab, gain_out, w_gate, w_out, cotangent = inputs
    recv_ab, held, came = beside(send_ab, LANES)
    recv_ab, held = lax.optimization_barrier((recv_ab, wide_in))
    send_b, a_own = call(spread_kernel, [(copies, BF16), ((WIDTH, 2 * WIDTH), BF16)], [], recv_ab)
    send_b, held, a_own, normed_in = lax.optimization_barrier((send_b, held, a_own, normed_in))
    prepared = call(
        prepare_kernel,
        [
            (flat, F32), ((PAIRS, 1), F32), (tall, BF16), ((4 * WIDTH, PAIRS), F32),
            (flat, F32), (flat, F32), ((WIDTH, 1), F32), (square, BF16),
        ],
        [pltpu.VMEM(flat, F32), pltpu.VMEM(square, F32)],
        pair, w_ab, normed_in, cotangent, w_gate, gain_out, w_out,
        cost=pl.CostEstimate(flops=150_000_000, bytes_accessed=3000000, transcendentals=200_000),
    )
    came, a_near = swap(held, *GATHER[0]), swap(a_own, "y", 1)
    b_all, held, came, a_own, a_near, prepared = lax.optimization_barrier(
        (exchange(send_b, SIDES), held, came, a_own, a_near, prepared)
    )
    h_in, inv_in, w_ab_own, factors, gate, cot, scale, w_out_own = prepared
    held = jnp.concatenate([held, came], axis=0)
    send_mixed, a_all = call(
        mix_kernel, [(flat, BF16), ((2 * WIDTH, 2 * WIDTH), BF16)], [], a_own, a_near, b_all
    )
    recv_mixed, held, came = beside(send_mixed, LANES, (held, *GATHER[1]))
    held = jnp.concatenate(held + came, axis=0)
    update, send_d, d_gate = call(
        middle_kernel,
        [(blocks, BF16), (twice, BF16), (flat, BF16)],
        [pltpu.VMEM(flat, F32), pltpu.VMEM(square, F32)],
        recv_mixed, normed_in, gate, cot, scale, w_out_own,
    )
    recv_d, held, came = beside(send_d, LANES, (held, *GATHER[2]))
    held = jnp.concatenate(held + came, axis=0)
    d_a_own, d_a_near, d_b = call(
        grad_kernel, [(flat, F32), (flat, BF16), (copies, BF16)], [], a_all, b_all, recv_d
    )
    d_b, (_, held), (d_a_near, came) = beside(d_b, SIDES, (d_a_near, "y", 1), (held, *GATHER[3]))
    wide_parts = [held, came]
    d_a, d_b, sums = call(
        weight_kernel,
        [(flat, F32), (flat, F32), ((NSIDE * SHARE, WIDTH), BF16)],
        [pltpu.VMEM((TAPS * ROWS, WIDTH), F32), pltpu.VMEM((TAPS * ROWS, WIDTH), F32)],
        *wide_parts, w_ab, d_a_own, d_a_near, d_b, recv_d,
    )
    sums = exchange(sums, SIDES)
    (send_last,) = call(join_kernel, [(last, BF16)], [], d_a, d_b, sums)
    recv_last = exchange(send_last, LANES)
    recv_near = swap(recv_last, "core", 1)
    (grad_pair,) = call(
        last_kernel,
        [(blocks, BF16)],
        [pltpu.VMEM(flat, F32), pltpu.VMEM(last, F32)],
        recv_last, pair_mask, gain_in, w_gate, d_gate, h_in, inv_in, w_ab_own, factors,
    )
    recv_near, grad_pair = lax.optimization_barrier((recv_near, grad_pair))
    grad_ab, grad_gate, grad_out = call(
        sums_kernel,
        [(wide, F32), (square, F32), (square, F32)],
        [pltpu.VMEM(tall, F32), pltpu.VMEM((NLANE * SHARE, WIDTH), F32)],
        recv_last, recv_near,
    )
    return update, grad_pair, grad_ab, grad_gate, grad_out


def solution(mesh):
    split = Mesh(mesh.devices.reshape(NROW, 8, 2, 2), ("row", "z", "y", "core"))
    cols = ("z", "y", "core")
    blocks = P("row", cols, None)
    placed = (blocks, P("row", cols), P(), P(), P(), P(), P(), blocks)
    return jax.shard_map(
        on_device,
        mesh=split,
        in_specs=placed,
        out_specs=(blocks, blocks, P(), P(), P()),
        check_vma=False,
    )
```

```python
import jax
import jax.numpy as jnp
from jax import lax
from jax.experimental import pallas as pl
from jax.experimental.pallas import tpu as pltpu
from jax.sharding import Mesh, PartitionSpec as P

F32 = jnp.float32
BF16 = jnp.bfloat16

ROWS, COLS, WIDTH = 32, 8, 128
NROW, NLANE, NSIDE = 8, 16, 16
PAIRS = ROWS * COLS
GROUP = WIDTH // NLANE
QUAD = WIDTH // ROWS
HALF = ROWS // 2
RES = 256
TAPS = 4 * GROUP
SHARE = TAPS + 2 * WIDTH // NLANE
FINAL = 4 * COLS + SHARE // 2
GATHER = (("z", 4), ("z", 2), ("core", 1), ("z", 1))


def dot(left, right, left_dim, right_dim):
    return lax.dot_general(
        left, right, (((left_dim,), (right_dim,)), ((), ())), preferred_element_type=F32
    )


def lane_block(shape, size=ROWS):
    return lax.broadcasted_iota(jnp.int32, shape, 1) // size


def load_pairs(block, scratch):
    scratch[...] = block[...].astype(F32).reshape(PAIRS, WIDTH)
    return jnp.concatenate(
        [scratch[pl.ds(k, ROWS, stride=COLS), :] for k in range(COLS)], axis=0
    )


def store_pairs(values, scratch, block):
    for k in range(COLS):
        scratch[pl.ds(k, ROWS, stride=COLS), :] = values[k * ROWS : (k + 1) * ROWS]
    block[...] = scratch[...].reshape(ROWS, COLS, WIDTH).astype(block.dtype)


def regroup(scratch, blocks):
    return jnp.concatenate(
        [
            scratch[pl.ds(blk * WIDTH + cc, NLANE, stride=GROUP), :]
            for blk in range(blocks)
            for cc in range(GROUP)
        ],
        axis=0,
    )


def ungroup(values, scratch):
    for cc in range(GROUP):
        scratch[pl.ds(cc, NLANE, stride=GROUP), :] = values[cc * NLANE : (cc + 1) * NLANE]


def moved(part, shift):
    shift = shift % WIDTH
    return pltpu.roll(part, shift, 1) if shift else part


def to_message(values, k, which, size):
    tile, start = k // QUAD, k % QUAD * ROWS
    first = which * QUAD
    if size == HALF:
        start, first = start + which * HALF, 0
    block = lane_block((NLANE, WIDTH), size)
    result = None
    for place in range(WIDTH // size):
        row = (first + place) * NLANE
        part = moved(values[row : row + NLANE, tile * WIDTH : (tile + 1) * WIDTH], place * size - start)
        result = part if result is None else jnp.where(block == place, part, result)
    return result


def from_message(pieces, size):
    block = lane_block((NLANE, WIDTH), size)
    bands = []
    for cc in range(GROUP):
        tiles = []
        for tile in range(COLS // QUAD):
            result = None
            for place in range(WIDTH // size):
                if size == ROWS:
                    part = pieces[tile * QUAD + place][cc // QUAD]
                    start = cc % QUAD * ROWS
                else:
                    part = pieces[tile * QUAD + place // 2][place % 2]
                    start = cc * HALF
                part = moved(part, place * size - start)
                result = part if result is None else jnp.where(block == place, part, result)
            tiles.append(result)
        bands.append(jnp.concatenate(tiles, axis=1))
    return jnp.concatenate(bands, axis=0)


def mask_rows(mask):
    flags = mask[...].astype(F32).astype(BF16)
    source = lax.broadcasted_iota(jnp.int32, (ROWS, WIDTH), 0)
    lane = lax.broadcasted_iota(jnp.int32, (ROWS, WIDTH), 1)
    return [
        dot(flags, (place == source).astype(F32).astype(BF16), 1, 0)
        for place in (lane % ROWS, lane % HALF, lane % HALF + HALF)
    ]


def column_of(gain):
    row = lax.broadcasted_iota(jnp.int32, (WIDTH, WIDTH), 0)
    lane = lax.broadcasted_iota(jnp.int32, (WIDTH, WIDTH), 1)
    here = lane == (row % NLANE) * GROUP + row // NLANE
    return jnp.sum(jnp.where(here, gain, 0.0), axis=1, keepdims=True)


def layer_norm(values, axis):
    center = values - jnp.mean(values, axis=axis, keepdims=True)
    inverse = lax.rsqrt(jnp.mean(center * center, axis=axis, keepdims=True) + 1e-05)
    return center * inverse, inverse


def norm_back(grad_h, normed, inverse, axis):
    first = jnp.mean(grad_h, axis=axis, keepdims=True)
    second = jnp.mean(grad_h * normed, axis=axis, keepdims=True)
    return inverse * (grad_h - first - normed * second)


def split_rows(message, parts):
    wide = message.astype(F32).reshape(NLANE, parts, COLS, WIDTH)
    return [wide[:, part].reshape(NLANE * COLS, WIDTH) for part in range(parts)]


def project_kernel(*refs):
    count = len(refs) - 7
    inputs, kept = refs[: count // 2], refs[count // 2 : count]
    normed_out, wide_out, send, rows, weights, message, sems = refs[count:]
    copies = [
        pltpu.make_async_copy(there, here, sems.at[place])
        for place, (there, here) in enumerate(zip(inputs, kept))
    ]
    for copy in copies:
        copy.start()
    pair_here, mask_here, gain_here, w_here = kept[:4]
    for copy in copies[:3]:
        copy.wait()
    h_in, _ = layer_norm(pair_here[...].astype(F32).reshape(PAIRS, WIDTH), 1)
    rows[...] = (h_in * gain_here[...]).astype(BF16).astype(F32)
    normed = jnp.concatenate(
        [rows[pl.ds(k, ROWS, stride=COLS), :] for k in range(COLS)], axis=0
    ).astype(BF16)
    normed_out[...] = normed
    flags, *half_flags = mask_rows(mask_here)
    wide_out[...] = jnp.concatenate(
        [rows[i * COLS : (i + 1) * COLS] * flags[:, i : i + 1] for i in range(ROWS)], axis=1
    ).astype(BF16)
    copies[3].wait()
    weights[...] = w_here[...].astype(F32).T
    proj = dot(regroup(weights, 4).astype(BF16), normed, 1, 1)
    a_val = jax.nn.sigmoid(proj[0:128]) * proj[128:256]
    b_val = jax.nn.sigmoid(proj[256:384]) * proj[384:512]
    for k in range(COLS):
        for part in range(2):
            message[pl.ds(part * COLS + k, NLANE, stride=4 * COLS), :] = (
                to_message(a_val, k, part, ROWS) * flags[k : k + 1]
            )
            message[pl.ds((2 + part) * COLS + k, NLANE, stride=4 * COLS), :] = (
                to_message(b_val, k, part, HALF) * half_flags[part][k : k + 1]
            )
    send[...] = message[...].astype(BF16)
    for copy in copies[4:]:
        copy.wait()


def spread_kernel(recv, send, a_own):
    parts = split_rows(recv[...], 4)
    a_own[...] = jnp.concatenate(parts[:2], axis=1).astype(BF16)
    for side in range(NSIDE):
        send[side * WIDTH : (side + 1) * WIDTH] = parts[2 + side % 2].astype(BF16)


def mix_kernel(own, near, b_all, send, a_all):
    is_first = lax.axis_index("y") == 0
    own, near = own[...], near[...]
    a_val = [jnp.where(is_first, own, near), jnp.where(is_first, near, own)]
    a_all[...] = jnp.concatenate(a_val, axis=0)
    block = lane_block((HALF, WIDTH))
    pieces = [[], []]
    for r in range(NROW):
        full = None
        for y in range(2):
            side = 2 * r + y
            term = dot(b_all[side * WIDTH : (side + 1) * WIDTH], a_val[y], 0, 0)
            full = term if full is None else full + term
        found = []
        for h in range(2):
            mixed = None
            for c4 in range(QUAD):
                row = (h * QUAD + c4) * HALF
                part = full[row : row + HALF, h * WIDTH : (h + 1) * WIDTH]
                mixed = part if mixed is None else jnp.where(block == c4, part, mixed)
            found.append(mixed)
        for core in range(2):
            pieces[core] += [found[h][core * COLS : (core + 1) * COLS] for h in range(2)]
    send[...] = jnp.concatenate(pieces[0] + pieces[1], axis=0).astype(BF16)


def prepare_kernel(
    pair, w_ab, normed_in, cotangent, w_gate, gain_out, w_out,
    h_in, inv_in, w_ab_own, factors, gate, cot, scale, w_out_own, rows, weights,
):
    h_in[...], inv_in[...] = layer_norm(load_pairs(pair, rows), 1)
    flat_in = normed_in[...]
    weights[...] = w_out[...].astype(F32)
    w_out_own[...] = regroup(weights, 1).astype(BF16)
    scale[...] = column_of(gain_out[...])
    gate[...] = jax.nn.sigmoid(dot(flat_in, w_gate[...], 1, 0))
    cot[...] = load_pairs(cotangent, rows)
    for blk in range(4):
        weights[...] = w_ab[:, blk * WIDTH : (blk + 1) * WIDTH].astype(F32).T
        w_ab_own[blk * WIDTH : (blk + 1) * WIDTH] = regroup(weights, 1).astype(BF16)
    proj = dot(w_ab_own[...], flat_in, 1, 1)
    for half in range(2):
        start = half * 2 * WIDTH
        sig = jax.nn.sigmoid(proj[start : start + WIDTH])
        value = proj[start + WIDTH : start + 2 * WIDTH]
        factors[start : start + WIDTH] = value * sig * (1.0 - sig)
        factors[start + WIDTH : start + 2 * WIDTH] = sig


def middle_kernel(
    recv, normed_in, gate, cot, scale, w_out_own,
    update, send, d_gate_out, rows, weights,
):
    rows[...] = recv[...].astype(F32)
    mixed = from_message(
        [
            [rows[pl.ds(h * COLS + k, NLANE, stride=2 * COLS), :] for h in range(2)]
            for k in range(COLS)
        ],
        ROWS,
    )
    h_out, inv_out = layer_norm(mixed, 0)
    scale = scale[...]
    normed = (h_out * scale).astype(BF16)
    w_own = w_out_own[...]
    y_val = dot(normed, w_own, 0, 0)
    flat_in = normed_in[...]
    gate, cot = gate[...], cot[...]
    store_pairs(gate * y_val, rows, update)
    d_y = (cot * gate).astype(BF16)
    d_gate = (cot * y_val * gate * (1.0 - gate)).astype(BF16)
    d_gate_out[...] = d_gate
    ungroup(dot(normed, d_y, 1, 0), weights)
    grad_h = dot(w_own, d_y, 1, 1) * scale
    d_mixed = norm_back(grad_h, h_out, inv_out, 0)
    for k in range(COLS):
        for h in range(2):
            rows[pl.ds(h * COLS + k, NLANE, stride=2 * COLS), :] = to_message(d_mixed, k, h, ROWS)
    sums = jnp.concatenate([dot(flat_in, d_gate, 0, 0), weights[...]], axis=0)
    both = jnp.concatenate(
        [rows[...].reshape(NLANE, 2 * COLS, WIDTH), sums.reshape(NLANE, 2 * COLS, WIDTH)], axis=1
    )
    send[...] = both.reshape(2 * PAIRS, WIDTH).astype(BF16)


def grad_kernel(a_all, b_all, recv_d, d_a_own, d_a_near, d_b):
    d_mixed = split_rows(recv_d[...], 4)[:2]
    a_val = [a_all[y * WIDTH : (y + 1) * WIDTH] for y in range(2)]
    block = lane_block((HALF, WIDTH))
    totals = [None, None]
    for r in range(NROW):
        tiles = []
        for h in range(2):
            part = jnp.concatenate(
                [d_mixed[h][at : at + COLS] for at in (r * COLS, (NROW + r) * COLS)], axis=0
            )
            nothing = jnp.zeros_like(part)
            tiles.append(
                jnp.concatenate(
                    [
                        jnp.where(block == cc % QUAD, part, nothing) if cc // QUAD == h else nothing
                        for cc in range(GROUP)
                    ],
                    axis=0,
                )
            )
        spread = jnp.concatenate(tiles, axis=1).astype(BF16)
        for y in range(2):
            side = 2 * r + y
            term = dot(b_all[side * WIDTH : (side + 1) * WIDTH], spread, 1, 0)
            totals[y] = term if totals[y] is None else totals[y] + term
            d_b[side * WIDTH : (side + 1) * WIDTH] = dot(a_val[y], spread, 1, 1).astype(BF16)
    is_first = lax.axis_index("y") == 0
    for h in range(2):
        first, second = (total[:, h * WIDTH : (h + 1) * WIDTH] for total in totals)
        d_a_own[h * WIDTH : (h + 1) * WIDTH] = jnp.where(is_first, first, second)
        d_a_near[h * WIDTH : (h + 1) * WIDTH] = jnp.where(is_first, second, first).astype(BF16)


def in_gather_order(values, lane):
    for bit in range(4):
        size = COLS << bit
        pairs = values.reshape(WIDTH // (2 * size), 2, size, WIDTH)
        swapped = jnp.concatenate([pairs[:, 1:], pairs[:, :1]], axis=1)
        values = jnp.where((lane >> bit) & 1 == 1, swapped, pairs).reshape(WIDTH, WIDTH)
    places = [0]
    for axis, step in GATHER:
        places += [place ^ (step if axis == "z" else 8 * step) for place in places]
    return jnp.concatenate([values[p * COLS : (p + 1) * COLS] for p in places], axis=0)


def weight_kernel(
    wide_0, wide_1, w_ab, d_a_own, d_a_near, d_b, recv_d, d_a_sum, d_b_sum, send, proj, d_proj
):
    lane = lax.axis_index("core") * 8 + lax.axis_index("z")
    d_a = d_a_own[...] + d_a_near[...].astype(F32)
    d_a_sum[...] = d_a
    totals = []
    for y in range(2):
        total = d_b[y * WIDTH : (y + 1) * WIDTH].astype(F32)
        for r in range(1, NROW):
            side = 2 * r + y
            total = total + d_b[side * WIDTH : (side + 1) * WIDTH].astype(F32)
        totals.append(total)
    d_b_sum[...] = jnp.concatenate(totals, axis=0)
    tall = 4 * WIDTH
    tap = lax.broadcasted_iota(jnp.int32, (tall, TAPS), 1)
    source = tap // GROUP * WIDTH + lane * GROUP + tap % GROUP
    pick = (lax.broadcasted_iota(jnp.int32, (tall, TAPS), 0) == source).astype(F32)
    w_own = dot(pick.astype(BF16), w_ab[...], 0, 1)
    nothing = jnp.zeros_like(w_own)
    w_twice = jnp.concatenate(
        [jnp.concatenate([w_own, nothing], axis=1), jnp.concatenate([nothing, w_own], axis=1)],
        axis=0,
    ).astype(BF16)
    parts = []
    for i in range(0, ROWS, 2):
        lanes = slice(i * WIDTH, (i + 2) * WIDTH)
        part = jnp.concatenate([wide_0[:, lanes], wide_1[:, lanes]], axis=0)
        parts.append(part)
        values = dot(w_twice, part, 1, 1)
        for odd in range(2):
            proj[pl.ds(i + odd, TAPS, stride=ROWS), :] = values[odd * TAPS : (odd + 1) * TAPS]
    turned_a = jnp.concatenate(
        [in_gather_order(d_a[h * WIDTH : (h + 1) * WIDTH], lane).T for h in range(2)], axis=0
    )
    sides = [in_gather_order(total, lane).T for total in totals]
    turned_b = jnp.concatenate(
        [side[cc * HALF : (cc + 1) * HALF] for cc in range(GROUP) for side in sides], axis=0
    )
    for half, d_val in enumerate((turned_a, turned_b)):
        start = half * 2 * RES
        sig = jax.nn.sigmoid(proj[start : start + RES])
        value = proj[start + RES : start + 2 * RES]
        d_value = d_val * sig
        d_proj[start : start + RES] = d_value * value * (1.0 - sig)
        d_proj[start + RES : start + 2 * RES] = d_value
    sums = None
    for i in range(0, ROWS, 2):
        left = jnp.concatenate(
            [d_proj[pl.ds(i + odd, TAPS, stride=ROWS), :] for odd in range(2)], axis=0
        ).astype(BF16)
        both = dot(left, parts[i // 2], 1, 0)
        term = both[:TAPS, :WIDTH] + both[TAPS:, WIDTH:]
        sums = term if sums is None else sums + term
    others = recv_d[...].astype(F32).reshape(NLANE, 4 * COLS, WIDTH)[:, 2 * COLS :]
    own = jnp.concatenate([sums, jnp.sum(others, axis=0)], axis=0) * (1.0 / RES)
    for side in range(NSIDE):
        send[side * SHARE : (side + 1) * SHARE] = own.astype(BF16)


def join_kernel(d_a, d_b, sums, send):
    total = jnp.sum(sums[...].astype(F32).reshape(NSIDE, SHARE, WIDTH), axis=0)
    pieces = [
        half[part * WIDTH : (part + 1) * WIDTH].reshape(NLANE, COLS, WIDTH)
        for half in (d_a, d_b)
        for part in range(2)
    ]
    shares = jnp.broadcast_to(
        total.reshape(2, 1, SHARE // 2, WIDTH), (2, NLANE // 2, SHARE // 2, WIDTH)
    )
    pieces.append(shares.reshape(NLANE, SHARE // 2, WIDTH))
    send[...] = jnp.concatenate(pieces, axis=1).reshape(NLANE * FINAL, WIDTH).astype(BF16)


def last_kernel(
    recv, mask, gain, w_gate, d_gate, h_in, inv_in, w_ab_own, factors,
    grad_pair, rows, message,
):
    w_own = w_ab_own[...]
    flags, *half_flags = mask_rows(mask)
    message[...] = recv[...].astype(F32)
    grads = []
    for half, size in enumerate((ROWS, HALF)):
        pieces = [
            [
                message[pl.ds((half * 2 + part) * COLS + k, NLANE, stride=FINAL), :]
                * (half_flags[part] if half else flags)[k : k + 1]
                for part in range(2)
            ]
            for k in range(COLS)
        ]
        d_val = from_message(pieces, size)
        start = half * 2 * WIDTH
        grads += [
            d_val * factors[start : start + WIDTH],
            d_val * factors[start + WIDTH : start + 2 * WIDTH],
        ]
    d_proj = jnp.concatenate(grads, axis=0).astype(BF16)
    d_in = dot(d_proj, w_own, 0, 0) + dot(d_gate[...], w_gate[...], 1, 1)
    store_pairs(norm_back(d_in * gain[...], h_in[...], inv_in[...], 1), rows, grad_pair)


def sums_kernel(
    recv, recv_near, grad_ab, grad_gate, grad_out, weights, message, turned, others, sems
):
    own, near = (
        part[...].astype(F32).reshape(NLANE, FINAL, WIDTH)[:, 4 * COLS :]
        for part in (recv, recv_near)
    )
    is_first = lax.axis_index("core") == 0
    both = [jnp.where(is_first, own, near), jnp.where(is_first, near, own)]
    both = jnp.concatenate(both, axis=1)
    others[...] = both[:, TAPS:].reshape(PAIRS, WIDTH)
    copies = [
        pltpu.make_async_copy(others.at[pl.ds(0, WIDTH)], grad_gate, sems.at[0]),
        pltpu.make_async_copy(others.at[pl.ds(WIDTH, WIDTH)], grad_out, sems.at[1]),
        pltpu.make_async_copy(turned, grad_ab, sems.at[2]),
    ]
    copies[0].start()
    copies[1].start()
    message[...] = both.reshape(NLANE * SHARE, WIDTH)
    for blk in range(4):
        for cc in range(GROUP):
            weights[pl.ds(blk * WIDTH + cc, NLANE, stride=GROUP), :] = message[
                pl.ds(blk * GROUP + cc, NLANE, stride=SHARE), :
            ]
    turned[...] = weights[...].T
    copies[2].start()
    for copy in copies:
        copy.wait()


def call(kernel, outs, scratch, *args, places=None, cost=None, apart=False):
    return pl.pallas_call(
        kernel,
        out_shape=[jax.ShapeDtypeStruct(shape, dtype) for shape, dtype in outs],
        in_specs=[
            pl.BlockSpec(memory_space=pltpu.VMEM if places is None else places[n])
            for n in range(len(args))
        ],
        out_specs=[pl.BlockSpec(memory_space=pl.ANY if apart else pltpu.VMEM) for _ in outs],
        scratch_shapes=scratch,
        compiler_params=pltpu.CompilerParams(vmem_limit_bytes=32 * 1024 * 1024),
        cost_estimate=cost,
    )(*args)


LANES = ("core", "z")
SIDES = ("row", "y")


def exchange(values, axes):
    return lax.all_to_all(values, axes, 0, 0, tiled=True)


def swap(values, axis, step):
    return lax.ppermute(values, axis, [(n, n ^ step) for n in range(lax.axis_size(axis))])


def beside(values, axes, *swaps):
    held = [array for array, _, _ in swaps]
    came = [swap(array, axis, step) for array, (_, axis, step) in zip(held, swaps)]
    return lax.optimization_barrier((exchange(values, axes), held, came))


def on_device(pair, pair_mask, ln_in_gain, w_ab, w_gate, ln_out_gain, w_out, cotangent):
    pair_mask = pair_mask.T
    gain_in = ln_in_gain.reshape(1, WIDTH)
    gain_out = ln_out_gain.reshape(1, WIDTH)
    flat = (PAIRS, WIDTH)
    twice = (2 * PAIRS, WIDTH)
    copies = (NSIDE * WIDTH, WIDTH)
    blocks = (ROWS, COLS, WIDTH)
    square = (WIDTH, WIDTH)
    wide = (WIDTH, 4 * WIDTH)
    tall = (4 * WIDTH, WIDTH)
    last = (NLANE * FINAL, WIDTH)
    inputs = (pair, pair_mask, gain_in, w_ab, gain_out, w_gate, w_out, cotangent)
    *inputs, normed_in, wide_in, send_ab = call(
        project_kernel,
        [(array.shape, array.dtype) for array in inputs]
        + [(flat, BF16), ((COLS, ROWS * WIDTH), BF16), (twice, BF16)],
        [
            pltpu.VMEM(flat, F32),
            pltpu.VMEM(tall, F32),
            pltpu.VMEM(twice, F32),
            pltpu.SemaphoreType.DMA((len(inputs),)),
        ],
        *(pltpu.with_memory_space_constraint(array, pltpu.HBM) for array in inputs),
        places=[pltpu.HBM] * len(inputs),
    )
    pair, pair_mask, gain_in, w_ab, gain_out, w_gate, w_out, cotangent = inputs
    recv_ab, held, came = beside(send_ab, LANES)
    recv_ab, held = lax.optimization_barrier((recv_ab, wide_in))
    send_b, a_own = call(spread_kernel, [(copies, BF16), ((WIDTH, 2 * WIDTH), BF16)], [], recv_ab)
    send_b, held, a_own, normed_in = lax.optimization_barrier((send_b, held, a_own, normed_in))
    prepared = call(
        prepare_kernel,
        [
            (flat, F32), ((PAIRS, 1), F32), (tall, BF16), ((4 * WIDTH, PAIRS), F32),
            (flat, F32), (flat, F32), ((WIDTH, 1), F32), (square, BF16),
        ],
        [pltpu.VMEM(flat, F32), pltpu.VMEM(square, F32)],
        pair, w_ab, normed_in, cotangent, w_gate, gain_out, w_out,
        cost=pl.CostEstimate(flops=150_000_000, bytes_accessed=3000000, transcendentals=200_000),
    )
    came, a_near = swap(held, *GATHER[0]), swap(a_own, "y", 1)
    b_all, held, came, a_own, a_near, prepared = lax.optimization_barrier(
        (exchange(send_b, SIDES), held, came, a_own, a_near, prepared)
    )
    h_in, inv_in, w_ab_own, factors, gate, cot, scale, w_out_own = prepared
    held = jnp.concatenate([held, came], axis=0)
    send_mixed, a_all = call(
        mix_kernel, [(flat, BF16), ((2 * WIDTH, 2 * WIDTH), BF16)], [], a_own, a_near, b_all
    )
    recv_mixed, held, came = beside(send_mixed, LANES, (held, *GATHER[1]))
    held = jnp.concatenate(held + came, axis=0)
    update, send_d, d_gate = call(
        middle_kernel,
        [(blocks, BF16), (twice, BF16), (flat, BF16)],
        [pltpu.VMEM(flat, F32), pltpu.VMEM(square, F32)],
        recv_mixed, normed_in, gate, cot, scale, w_out_own,
    )
    recv_d, held, came = beside(send_d, LANES, (held, *GATHER[2]))
    held = jnp.concatenate(held + came, axis=0)
    d_a_own, d_a_near, d_b = call(
        grad_kernel, [(flat, F32), (flat, BF16), (copies, BF16)], [], a_all, b_all, recv_d
    )
    d_b, (_, held), (d_a_near, came) = beside(d_b, SIDES, (d_a_near, "y", 1), (held, *GATHER[3]))
    wide_parts = [held, came]
    d_a, d_b, sums = call(
        weight_kernel,
        [(flat, F32), (flat, F32), ((NSIDE * SHARE, WIDTH), BF16)],
        [pltpu.VMEM((TAPS * ROWS, WIDTH), F32), pltpu.VMEM((TAPS * ROWS, WIDTH), F32)],
        *wide_parts, w_ab, d_a_own, d_a_near, d_b, recv_d,
    )
    sums = exchange(sums, SIDES)
    (send_last,) = call(join_kernel, [(last, BF16)], [], d_a, d_b, sums)
    recv_last = exchange(send_last, LANES)
    recv_near = swap(recv_last, "core", 1)
    (grad_pair,) = call(
        last_kernel,
        [(blocks, BF16)],
        [pltpu.VMEM(flat, F32), pltpu.VMEM(last, F32)],
        recv_last, pair_mask, gain_in, w_gate, d_gate, h_in, inv_in, w_ab_own, factors,
    )
    recv_near, grad_pair = lax.optimization_barrier((recv_near, grad_pair))
    grad_ab, grad_gate, grad_out = call(
        sums_kernel,
        [(wide, F32), (square, F32), (square, F32)],
        [
            pltpu.VMEM(tall, F32),
            pltpu.VMEM((NLANE * SHARE, WIDTH), F32),
            pltpu.VMEM(wide, F32),
            pltpu.VMEM(flat, F32),
            pltpu.SemaphoreType.DMA((3,)),
        ],
        recv_last, recv_near,
        apart=True,
    )
    return update, grad_pair, grad_ab, grad_gate, grad_out


def solution(mesh):
    split = Mesh(mesh.devices.reshape(NROW, 8, 2, 2), ("row", "z", "y", "core"))
    cols = ("z", "y", "core")
    blocks = P("row", cols, None)
    placed = (blocks, P("row", cols), P(), P(), P(), P(), P(), blocks)
    return jax.shard_map(
        on_device,
        mesh=split,
        in_specs=placed,
        out_specs=(blocks, blocks, P(), P(), P()),
        check_vma=False,
    )
```
